32 devices in a mesh: pipe: 2 (over core), fsdp: 4 (over z), tensor: 4 (over y, x).
Axes of the slice: x: 2, y: 2, z: 4, core: 2. Of those that a mesh axis runs over, the one named last changes fastest.
Arguments:
- tokens: bfloat16 [2, 4096, 1536], P(None, ('fsdp', 'tensor')), may hold values from -6 to 6
- out_grad: bfloat16 [2, 4096, 1536], P(None, ('fsdp', 'tensor')), may hold values from -6 to 6
- seq_lengths: int32 [2, 4, 3], P(None, 'fsdp'), may hold values from 1 to 1022, as said below
- norm_gain: bfloat16 [2, 1536], P('pipe', 'fsdp'), may hold values from 0.5 to 1.5
- w_zx: bfloat16 [2, 1536, 2, 3072], P('pipe', 'fsdp', None, 'tensor'), may hold values from -0.15625 to 0.15625
- w_bc: bfloat16 [2, 1536, 256], P('pipe', 'fsdp'), may hold values from -0.15625 to 0.15625
- w_dt: bfloat16 [2, 1536, 48], P('pipe', 'fsdp', 'tensor'), may hold values from -0.15625 to 0.15625
- conv_x: bfloat16 [2, 5, 48, 64], P('pipe', None, 'tensor', 'fsdp'), may hold values from -0.5 to 0.5
- conv_bc: bfloat16 [2, 5, 256], P('pipe', None, 'fsdp'), may hold values from -0.5 to 0.5
- out_gain: bfloat16 [2, 48, 64], P('pipe', 'tensor', 'fsdp'), may hold values from 0.5 to 1.5
- head_params: float32 [2, 3, 48], P('pipe', None, 'tensor'), may hold values from -4 to 1.5, as said below
- out_weight: bfloat16 [2, 3072, 1536], P('pipe', 'tensor', 'fsdp'), may hold values from -0.109375 to 0.109375
Outputs:
- section_outputs: bfloat16 [2, 2, 4096, 1536], P('pipe', None, ('fsdp', 'tensor'))
- input_grads: bfloat16 [2, 2, 4096, 1536], P('pipe', None, ('fsdp', 'tensor'))
- grad_norm_gain: float32 [2, 1536], P('pipe', ('fsdp', 'tensor'))
- grad_w_zx: float32 [2, 1536, 2, 3072], P('pipe', 'fsdp', None, 'tensor')
- grad_w_bc: float32 [2, 1536, 256], P('pipe', ('fsdp', 'tensor'))
- grad_w_dt: float32 [2, 1536, 48], P('pipe', 'fsdp', 'tensor')
- grad_conv_x: float32 [2, 5, 48, 64], P('pipe', None, 'tensor', 'fsdp')
- grad_conv_bc: float32 [2, 5, 256], P('pipe', None, ('fsdp', 'tensor'))
- grad_out_gain: float32 [2, 48, 64], P('pipe', 'tensor', 'fsdp')
- grad_head_params: float32 [2, 3, 48], P('pipe', None, 'tensor')
- grad_out_weight: float32 [2, 3072, 1536], P('pipe', 'tensor', 'fsdp')
The draws below stay inside these ranges and needn't reach their ends.
Inputs may be any that keep to these rules, and one draw needn't show every extreme that they name: `seq_lengths`: each row of 3 lengths sums to 1024; the first and the last are under 1024 / 8, so the middle sequence starts in the first 128 rows of its group and ends in the last; in data group 0 of every micro-batch the first and the last are 1. `head_params`: row 0 between -4 and -1, row 1 between -4 and 1.5, row 2 between 0.5 and 1.5.
All inputs are finite; a program needn't handle non-finite values.
Results may differ from the reference program's by a relative error of at most 0.028.
Values may be sent and summed in bfloat16 or wider, within the bound.
No kernel may reach another device: no remote copies, remote signals or barrier semaphores. Data moves between devices by JAX's collectives and lax.ppermute only.
A program may use at most 256 MiB of HBM per device.

```python
import jax
import jax.numpy as jnp
from jax import lax

D = 1536
HEADS = 48
HEADDIM = 64
STATE = 128
CONV = 4
STRETCH = 256
CAP = 1024
SEQS = 3
MICRO = 2
INNER = 3072
BLOCKS = 4
TOKENS = 4096
N_PIPE = 2
N_FSDP = 4


def draw_seq_lengths(key, part):
    key = jax.random.fold_in(key, 5)
    first_key, last_key = jax.random.split(key)
    group_count = TOKENS // CAP
    first_len = jax.random.randint(first_key, (MICRO, group_count, 1), 1, CAP // 8)
    last_len = jax.random.randint(last_key, (MICRO, group_count, 1), 1, CAP // 8)
    first_len = first_len.at[:, 0, :].set(1)
    last_len = last_len.at[:, 0, :].set(1)
    middle_len = CAP - first_len - last_len
    return jnp.concatenate([first_len, middle_len, last_len], axis=2).astype(jnp.int32)


def draw_head_params(key, part):
    key = jax.random.fold_in(key, 9)
    key_bias, key_rate, key_skip = jax.random.split(key, 3)
    shape = (2, 1, HEADS)
    step_bias = jax.random.uniform(key_bias, shape, jnp.float32, -4.0, -1.0)
    log_rate = jax.random.uniform(key_rate, shape, jnp.float32, -4.0, 1.5)
    skip_gain = jax.random.uniform(key_skip, shape, jnp.float32, 0.5, 1.5)
    return jnp.concatenate([step_bias, log_rate, skip_gain], axis=1)


def levels(own_key, dims, cuts, smallest, top_value):
    gain = 1.0
    for axis_at, shards_of in cuts:
        steps = jax.random.uniform(jax.random.fold_in(jax.random.fold_in(own_key, 6), axis_at), (shards_of,), jnp.float32, smallest / len(cuts), top_value / len(cuts))
        gain = gain * jnp.repeat(jnp.exp(steps), dims[axis_at] // shards_of).reshape((-1,) + (1,) * (len(dims) - 1 - axis_at))
    return gain


def centred(stream_key, dims, deviation, limit, cuts=(), kind=jnp.bfloat16):
    level = levels(stream_key, dims, cuts, -0.22, 0.18) if cuts else 1.0
    result = jax.random.normal(stream_key, dims, jnp.float32) * deviation * level
    return jnp.minimum(jnp.maximum(result, -limit), limit).astype(kind)


def setup_inputs(seed: int = 0) -> dict:
    seeds = jax.random.split(jax.random.key(seed), 13)
    return {
        "tokens": centred(seeds[0], (MICRO, TOKENS, D), 1.0, 6.0, ((1, 16),)),
        "out_grad": centred(seeds[1], (MICRO, TOKENS, D), 1.0, 6.0, ((1, 16),)),
        "seq_lengths": draw_seq_lengths(jax.random.fold_in(seeds[12], 71), 0),
        "norm_gain": jnp.clip(1.0 + 0.1 * jax.random.normal(seeds[3], (N_PIPE, D), jnp.float32), 0.5, 1.5).astype(jnp.bfloat16),
        "w_zx": centred(seeds[4], (N_PIPE, D, 2, INNER), D ** -0.5, 0.15625, ((0, 2), (1, 4), (3, 4))),
        "w_bc": centred(seeds[5], (N_PIPE, D, 2 * STATE), D ** -0.5, 0.15625, ((0, 2), (1, 4))),
        "w_dt": centred(seeds[6], (N_PIPE, D, HEADS), D ** -0.5, 0.15625, ((0, 2), (1, 4), (2, 4))),
        "conv_x": jnp.clip(jax.random.uniform(seeds[7], (N_PIPE, CONV + 1, HEADS, HEADDIM), jnp.float32, -0.5, 0.5) * levels(seeds[7], (N_PIPE, CONV + 1, HEADS, HEADDIM), ((0, 2), (2, 4), (3, 4)), -0.4, 0.0), -0.5, 0.5).astype(jnp.bfloat16),
        "conv_bc": jnp.clip(jax.random.uniform(seeds[8], (N_PIPE, CONV + 1, 2 * STATE), jnp.float32, -0.5, 0.5) * levels(seeds[8], (N_PIPE, CONV + 1, 2 * STATE), ((0, 2), (2, 4)), -0.4, 0.0), -0.5, 0.5).astype(jnp.bfloat16),
        "out_gain": jnp.clip(1.0 + 0.1 * jax.random.normal(seeds[9], (N_PIPE, HEADS, HEADDIM), jnp.float32), 0.5, 1.5).astype(jnp.bfloat16),
        "head_params": draw_head_params(jax.random.fold_in(seeds[12], 71), 0),
        "out_weight": centred(seeds[11], (N_PIPE, INNER, D), INNER ** -0.5, 0.109375, ((0, 2), (1, 4), (2, 4))),
    }


NORM_EPSILON = 1e-05

@jax.custom_vjp
def low(v):
    return lax.optimization_barrier(v.astype(jnp.bfloat16)).astype(jnp.float32)

@jax.custom_vjp
def low_back(v):
    return v

def low_keep(v):
    return (low(v), None)

def low_pass(kept, grad):
    return (grad,)

def back_keep(v):
    return (v, None)

def back_low(kept, grad):
    return (low(grad),)
low.defvjp(low_keep, low_pass)
low_back.defvjp(back_keep, back_low)

def segment_rows(lengths, row_count):
    seq_ends = jnp.cumsum(lengths).astype(jnp.int32)
    starts = (seq_ends - lengths).astype(jnp.int32)
    positions = jnp.arange(row_count, dtype=jnp.int32)
    segment = lax.optimization_barrier(jnp.sum((positions[:, None] >= seq_ends[None, :]).astype(jnp.int32), axis=1)).astype(jnp.int32)
    member = (segment[:, None] == jnp.arange(lengths.shape[0], dtype=jnp.int32)[None, :]).astype(jnp.int32)
    inside = (positions - lax.optimization_barrier(jnp.sum(member * starts[None, :], axis=1))).astype(jnp.int32)
    return (segment, inside)

def rms_norm(row_block, gain_vec):
    return row_block * lax.rsqrt(lax.optimization_barrier(jnp.mean(row_block * row_block, axis=1, keepdims=True)) + NORM_EPSILON) * gain_vec

def mixer_local(gate_in, conv_in, shared_in, step_in, conv_taps, shared_taps, head_vals, segment, inside, block_rows):
    row_count, inner_width = conv_in.shape
    head_count = step_in.shape[1]
    head_size = inner_width // head_count
    state_size = shared_in.shape[1] // 2
    tap_count = conv_taps.shape[0] - 1
    joined = jnp.concatenate([conv_in, shared_in], axis=1)
    filters = jnp.concatenate([conv_taps.reshape(tap_count + 1, inner_width), shared_taps], axis=1)
    conv_out = jnp.zeros_like(joined) + filters[tap_count]
    for lag_rows in range(tap_count):
        shifted = jnp.pad(joined, ((lag_rows, 0), (0, 0)))[:row_count]
        within = (inside >= lag_rows).astype(joined.dtype)[:, None]
        conv_out = conv_out + filters[tap_count - 1 - lag_rows] * shifted * within
    activated = jax.nn.silu(conv_out)
    values = activated[:, :inner_width].reshape(row_count, head_count, head_size)
    inputs_b = activated[:, inner_width:inner_width + state_size]
    outputs_c = activated[:, inner_width + state_size:]
    step_size = jax.nn.softplus(step_in + head_vals[0])
    log_decay = -step_size * jnp.exp(head_vals[1])
    scaled = values * step_size[:, :, None]
    block_count = row_count // block_rows
    positions = jnp.arange(block_rows, dtype=jnp.int32)
    lower_mask = positions[:, None] >= positions[None, :]
    lower_ones = lower_mask.astype(joined.dtype)

    def block_step(carried, block_items):
        held_state, previous = carried
        b_block, c_block, x_block, decay_block, seg_block = block_items
        cumulative = jnp.dot(lower_ones, decay_block, precision=lax.Precision.HIGHEST)
        across = cumulative.T
        same_seq = ((seg_block[:, None] == seg_block[None, :]) & lower_mask)[None, :, :]
        gap_logs = across[:, :, None] - across[:, None, :]
        weights = jnp.where(same_seq, jnp.exp(jnp.where(same_seq, gap_logs, 0.0)), 0.0)
        intersection = jnp.dot(c_block, b_block.T, precision=lax.Precision.HIGHEST)
        local_out = jnp.einsum('hij,jhp->ihp', weights * intersection[None, :, :], x_block, precision=lax.Precision.HIGHEST)
        carried_on = (seg_block == previous).astype(x_block.dtype)
        start_scale = jnp.exp(cumulative) * carried_on[:, None]
        from_state = jnp.einsum('in,hpn->ihp', c_block, held_state, precision=lax.Precision.HIGHEST) * start_scale[:, :, None]
        final_seg = seg_block[block_rows - 1].astype(jnp.int32)
        ending = jnp.exp(cumulative[block_rows - 1][None, :] - cumulative) * (seg_block == final_seg).astype(x_block.dtype)[:, None]
        fresh_state = jnp.einsum('jh,jhp,jn->hpn', ending, x_block, b_block, precision=lax.Precision.HIGHEST)
        kept_scale = jnp.exp(cumulative[block_rows - 1]) * (final_seg == previous).astype(x_block.dtype)
        held_state = fresh_state + kept_scale[:, None, None] * held_state
        return ((held_state, final_seg), local_out + from_state)
    start_carry = (jnp.zeros((head_count, head_size, state_size), joined.dtype), jnp.array(-1, jnp.int32))
    block_items = (inputs_b.reshape(block_count, block_rows, state_size), outputs_c.reshape(block_count, block_rows, state_size), scaled.reshape(block_count, block_rows, head_count, head_size), log_decay.reshape(block_count, block_rows, head_count), segment.reshape(block_count, block_rows))
    final_carry, outputs = lax.scan(jax.checkpoint(block_step), start_carry, block_items)
    total = outputs.reshape(row_count, head_count, head_size) + head_vals[2][None, :, None] * values
    return total.reshape(row_count, inner_width) * jax.nn.silu(gate_in)

def layer(params, x_rows, segment, inside):
    gain_vec, w_zx, w_bc, w_dt, conv_x, conv_bc, out_gain, head_params, out_weight = params
    normed = low(rms_norm(x_rows, gain_vec))
    shared_all = jnp.dot(normed, w_bc, precision=lax.Precision.HIGHEST)
    inner_width = INNER // BLOCKS
    group_heads = HEADS // BLOCKS
    mixed_list = []
    for block_index in range(BLOCKS):
        cols = slice(block_index * inner_width, (block_index + 1) * inner_width)
        heads_here = slice(block_index * group_heads, (block_index + 1) * group_heads)
        gate_in = low_back(jnp.dot(normed, w_zx[:, 0, cols], precision=lax.Precision.HIGHEST))
        conv_in = low_back(jnp.dot(normed, w_zx[:, 1, cols], precision=lax.Precision.HIGHEST))
        step_in = low_back(jnp.dot(normed, w_dt[:, heads_here], precision=lax.Precision.HIGHEST))
        mixed_list.append(mixer_local(gate_in, conv_in, low_back(shared_all), step_in, conv_x[:, heads_here], conv_bc, head_params[:, heads_here], segment, inside, STRETCH))
    squares = lax.optimization_barrier(jnp.sum(mixed_list[0] * mixed_list[0], axis=1))
    for block_index in range(1, BLOCKS):
        squares = squares + lax.optimization_barrier(jnp.sum(mixed_list[block_index] * mixed_list[block_index], axis=1))
    scale_rows = lax.rsqrt(squares / INNER + NORM_EPSILON)
    out_sum = jnp.zeros_like(x_rows)
    for block_index in range(BLOCKS):
        cols = slice(block_index * inner_width, (block_index + 1) * inner_width)
        heads_here = slice(block_index * group_heads, (block_index + 1) * group_heads)
        hidden = low(mixed_list[block_index] * scale_rows[:, None] * out_gain[heads_here].reshape(inner_width))
        out_sum = out_sum + low(jnp.dot(hidden, out_weight[cols], precision=lax.Precision.HIGHEST))
    return x_rows + low_back(out_sum)

def chain(first_input, zero_rows, first_params, second_params, segment, inside):
    first_out = layer(first_params, first_input, segment, inside)
    second_input = low(low_back(first_out)) + zero_rows
    second_out = layer(second_params, second_input, segment, inside)
    return (second_out, first_out)

def reference(tokens, out_grad, seq_lengths, norm_gain, w_zx, w_bc, w_dt, conv_x, conv_bc, out_gain, head_params, out_weight):
    params = tuple((array.astype(jnp.float32) for array in (norm_gain, w_zx, w_bc, w_dt, conv_x, conv_bc, out_gain, head_params, out_weight)))
    buffer_count = MICRO * N_FSDP
    flat_tokens = tokens.reshape(buffer_count, CAP, D)
    flat_grads = out_grad.reshape(buffer_count, CAP, D)
    flat_lengths = seq_lengths.reshape(buffer_count, SEQS)
    first_params = tuple((array[0] for array in params))
    second_params = tuple((array[1] for array in params))

    def one_buffer(totals, buffer_items):
        input_rows, cotangent, lengths = buffer_items
        segment, inside = segment_rows(lengths, CAP)

        def wrapped(first_input, zero_rows, first_weights, second_weights):
            return chain(first_input, zero_rows, first_weights, second_weights, segment, inside)
        second_out, pull_back, first_out = jax.vjp(wrapped, input_rows.astype(jnp.float32), jnp.zeros((CAP, D), jnp.float32), first_params, second_params, has_aux=True)
        grad_first, grad_second, grads_one, grads_two = pull_back(cotangent.astype(jnp.float32))
        totals = jax.tree.map(lambda total, part_one, part_two: total + jnp.stack([part_one, part_two]), totals, grads_one, grads_two)
        return (totals, (first_out.astype(jnp.bfloat16), second_out.astype(jnp.bfloat16), grad_first.astype(jnp.bfloat16), grad_second.astype(jnp.bfloat16)))
    start_totals = jax.tree.map(jnp.zeros_like, params)
    totals, stacked = lax.scan(one_buffer, start_totals, (flat_tokens, flat_grads, flat_lengths))
    first_out, second_out, grad_first, grad_second = stacked
    section_outputs = jnp.stack([first_out.reshape(MICRO, TOKENS, D), second_out.reshape(MICRO, TOKENS, D)])
    input_grads = jnp.stack([grad_first.reshape(MICRO, TOKENS, D), grad_second.reshape(MICRO, TOKENS, D)])
    grad_gain, grad_zx, grad_bc, grad_dt, grad_convx, grad_convbc, grad_outgain, grad_heads, grad_outw = totals
    return (section_outputs, input_grads, grad_gain, grad_zx, grad_bc, grad_dt, grad_convx, grad_convbc, grad_outgain, grad_heads, grad_outw)
```

```python
import jax
import jax.numpy as jnp
from jax import lax
from jax.experimental import pallas as pl
from jax.experimental.pallas import tpu as pltpu
from jax.sharding import PartitionSpec as P

STATE = 128
CHUNK = 256
HALF = 128
LANES = 128
NORM_EPSILON = 1e-05
LOG2E = 1.4426950408889634
F32 = jnp.float32
BF16 = jnp.bfloat16
VMEM_LIMIT = 56 * 1024 * 1024


def dot(a, b):
    return lax.dot_general(a, b, (((1,), (0,)), ((), ())), preferred_element_type=F32)


def dot_nt(a, b):
    return lax.dot_general(a, b, (((1,), (1,)), ((), ())), preferred_element_type=F32)


def dot_tn(a, b):
    return lax.dot_general(a, b, (((0,), (0,)), ((), ())), preferred_element_type=F32)


def pieces(value, count):
    found = []
    for _ in range(count):
        part = value.astype(BF16)
        found.append(part)
        value = value - part.astype(F32)
    return found


def dot_exact(ones, value):
    first, second, third = pieces(value, 3)
    return dot(ones, first) + (dot(ones, second) + dot(ones, third))


def spread(value, expander):
    first, second = pieces(value, 2)
    return dot(first, expander) + dot(second, expander)


def sigmoid(value):
    return 0.5 * jnp.tanh(0.5 * value) + 0.5


def softplus(value):
    return jnp.maximum(value, 0.0) + jnp.log1p(jnp.exp(-jnp.abs(value)))


def iota(shape, axis):
    return lax.broadcasted_iota(jnp.int32, shape, axis)


def segment_of(rows, first_end, second_end):
    return (rows >= first_end).astype(jnp.int32) + (rows >= second_end).astype(jnp.int32)


def head_expander(width):
    size = (LANES, width)
    return (iota(size, 0) == iota(size, 1) // 64).astype(BF16)


def head_folder(width):
    size = (width, LANES)
    return (iota(size, 1) == iota(size, 0) // 64).astype(BF16)


def lower_ones():
    size = (CHUNK, CHUNK)
    return (iota(size, 0) >= iota(size, 1)).astype(BF16)


def upper_ones():
    size = (CHUNK, CHUNK)
    return (iota(size, 0) <= iota(size, 1)).astype(BF16)


def decays(raw, head_ref, base, first_end, second_end, chunk):
    pre = raw + head_ref[0:1, :]
    step = softplus(pre)
    log_decay = -step * head_ref[1:2, :]
    total = dot_exact(lower_ones(), log_decay) * LOG2E
    rows = base + iota((CHUNK, LANES), 0)
    segment = segment_of(rows, first_end, second_end)
    previous = jnp.where(chunk == 0, -1, segment_of(base - 1, first_end, second_end))
    final = segment_of(base + CHUNK - 1, first_end, second_end)
    last = total[CHUNK - 1 : CHUNK, :]
    start = jnp.where(segment == previous, jnp.exp2(total), 0.0)
    ending = jnp.where(segment == final, jnp.exp2(last - total), 0.0)
    kept = jnp.where(final == previous, jnp.exp2(last), 0.0)
    return pre, step, log_decay, total, start, ending, kept


def same_block(row_base, col_base, first_end, second_end):
    size = (HALF, HALF)
    rows = row_base + iota(size, 0)
    cols = col_base + iota(size, 1)
    return (
        (segment_of(rows, first_end, second_end) == segment_of(cols, first_end, second_end)),
        rows,
        cols,
    )


def forward_kernel(
    scalars,
    x_ref,
    own_ref,
    other_ref,
    step_ref,
    out_own_ref,
    out_other_ref,
    taps_ref,
    gain_ref,
    skip_ref,
    head_ref,
    *rest,
):
    with_grad = len(rest) == 17
    rest = list(rest)
    grad_ref = rest.pop(0) if with_grad else None
    (
        part_ref,
        sums_ref,
        z_ref,
        conv_ref,
        input_ref,
        y_ref,
        raw_ref,
        state_ref,
        joined,
        state,
        hidden,
        end_x,
        from_state,
        step_wide,
        start_wide,
        end_wide,
    ) = rest
    chunk = pl.program_id(0)
    side, first_end, second_end = scalars[0], scalars[1], scalars[2]
    base = chunk * CHUNK
    width = hidden.shape[1]
    half = width // 2

    @pl.when(chunk == 0)
    def _():
        state[...] = jnp.zeros_like(state)
        joined[0:8, :] = jnp.zeros((8, joined.shape[1]), F32)

    x = x_ref[0]
    own = dot(x, own_ref[...])
    other = dot(x, other_ref[...])
    raw = dot(x, step_ref[...])
    raw_ref[0] = raw
    z_ref[0, :, :half] = own[:, :half].astype(BF16)
    z_ref[0, :, half:] = other[:, :half].astype(BF16)
    joined[8:, :half] = own[:, half:width]
    joined[8:, half:width] = other[:, half:width]
    joined[8:, width : width + STATE] = jnp.where(side == 0, own[:, width:], other[:, width:])
    joined[8:, width + STATE :] = jnp.where(side == 0, other[:, width:], own[:, width:])

    _, step, _, total, start, ending, kept = decays(
        raw, head_ref, base, first_end, second_end, chunk
    )
    expander = head_expander(width)
    step_wide[...] = spread(step, expander)
    start_wide[...] = spread(start, expander)
    end_wide[...] = spread(ending, expander)
    kept_wide = spread(jnp.broadcast_to(kept, (8, LANES)), expander)[0:1]
    total_rows = total.T

    rows = base + iota((CHUNK, LANES), 0)
    inside = rows - jnp.where(
        rows >= second_end, second_end, jnp.where(rows >= first_end, first_end, 0)
    )
    masks = [(inside >= lag).astype(F32) for lag in range(1, 4)]

    def activate(lanes):
        current = joined[8:, lanes]
        found = taps_ref[4:5, lanes] + taps_ref[3:4, lanes] * current
        for lag in range(1, 4):
            shifted = joined[8 - lag : 8 - lag + CHUNK, lanes] * masks[lag - 1]
            found = found + taps_ref[3 - lag : 4 - lag, lanes] * shifted
        conv_ref[0, :, lanes] = found.astype(BF16)
        input_ref[0, :, lanes] = current.astype(BF16)
        return found * sigmoid(found)

    b_f32 = activate(slice(width, width + STATE))
    b_low = b_f32.astype(BF16)
    c_low = activate(slice(width + STATE, width + 2 * STATE)).astype(BF16)
    state_ref[0] = state[...].astype(BF16)
    from_state[...] = dot(c_low, state[...].astype(BF16))
    inter = dot_nt(c_low, b_low)

    def masked(row_at, col_at):
        same, row_ids, col_ids = same_block(base + row_at, base + col_at, first_end, second_end)
        if row_at == col_at:
            same = same & (row_ids >= col_ids)
        return jnp.where(same, inter[row_at : row_at + HALF, col_at : col_at + HALF], 0.0)

    inter_00, inter_10, inter_11 = masked(0, 0), masked(HALF, 0), masked(HALF, HALF)
    low_lanes = iota((CHUNK, LANES), 1) < 64
    squares = jnp.zeros((CHUNK, LANES), F32)
    for tile in range(width // LANES):
        lanes = slice(tile * LANES, (tile + 1) * LANES)
        values = activate(lanes)
        scaled = values * step_wide[:, lanes]
        end_x[:, lanes] = (scaled * end_wide[:, lanes]).astype(BF16)
        scaled_parts = [
            jnp.where(low_lanes, scaled, 0.0).astype(BF16),
            jnp.where(low_lanes, 0.0, scaled).astype(BF16),
        ]
        top, bottom = [], []
        for side_at in range(2):
            head = 2 * tile + side_at
            column = total[:, head : head + 1]
            row = total_rows[head : head + 1, :]
            top_col, low_col = column[:HALF], column[HALF:]
            top_row, low_row = row[:, :HALF], row[:, HALF:]
            top.append((inter_00 * jnp.exp2(jnp.minimum(top_col - top_row, 0.0))).astype(BF16))
            bottom.append((inter_10 * jnp.exp2(low_col - top_row)).astype(BF16))
            bottom.append((inter_11 * jnp.exp2(jnp.minimum(low_col - low_row, 0.0))).astype(BF16))
        local_top = dot(
            jnp.concatenate(top, axis=1),
            jnp.concatenate([scaled_parts[0][:HALF], scaled_parts[1][:HALF]], axis=0),
        )
        local_bottom = dot(
            jnp.concatenate(bottom, axis=1), jnp.concatenate(scaled_parts, axis=0)
        )
        local = jnp.concatenate([local_top, local_bottom], axis=0)
        y = local + from_state[:, lanes] * start_wide[:, lanes] + skip_ref[0:1, lanes] * values
        y_ref[0, :, lanes] = y.astype(BF16)
        z = z_ref[0, :, lanes].astype(F32)
        mixed = y * (z * sigmoid(z))
        squares = squares + mixed * mixed
        hidden[:, lanes] = (mixed * gain_ref[0:1, lanes]).astype(BF16)
    state[...] = kept_wide * state[...] + dot(b_f32.T.astype(BF16), end_x[...])
    joined[0:8, :] = joined[CHUNK : CHUNK + 8, :]
    part = dot(hidden[:, :half], out_own_ref[...]) + dot(hidden[:, half:], out_other_ref[...])
    part_ref[0] = part.astype(BF16)
    ones = jnp.ones((8, LANES), BF16)
    first, second = pieces(squares, 2)
    square_rows = dot_nt(ones, first) + dot_nt(ones, second)
    if with_grad:
        crossed = jnp.zeros((CHUNK, LANES), F32)
        for tile in range(part.shape[1] // LANES):
            lanes = slice(tile * LANES, (tile + 1) * LANES)
            crossed = crossed + part[:, lanes] * grad_ref[0, :, lanes].astype(F32)
        first, second = pieces(crossed, 2)
        cross_rows = dot_nt(ones, first) + dot_nt(ones, second)
        square_rows = jnp.where(iota((8, CHUNK), 0) == 0, square_rows, cross_rows)
    sums_ref[...] = square_rows


def backward_kernel(
    scalars,
    grad_ref,
    rows_ref,
    own_ref,
    other_ref,
    step_ref,
    out_own_ref,
    out_other_ref,
    taps_ref,
    gain_ref,
    skip_ref,
    head_ref,
    z_ref,
    conv_ref,
    input_ref,
    y_ref,
    raw_ref,
    state_ref,
    back_ref,
    own_grad_ref,
    other_grad_ref,
    step_grad_ref,
    hidden_ref,
    taps_grad_ref,
    wide_grad_ref,
    head_grad_ref,
    grad_state,
    grad_conv,
    grad_y,
    grad_y_low,
    step_wide,
    start_wide,
    end_wide,
    from_state,
    to_state,
    end_x,
    start_dy,
    sum_end,
    sum_start,
    sum_step,
    grad_inter,
):
    turn = pl.program_id(0)
    chunk = pl.num_programs(0) - 1 - turn
    side, first_end, second_end = scalars[0], scalars[1], scalars[2]
    base = chunk * CHUNK
    width = hidden_ref.shape[2]
    half = width // 2

    @pl.when(turn == 0)
    def _():
        grad_state[...] = jnp.zeros_like(grad_state)
        grad_conv[CHUNK:, :] = jnp.zeros((8, grad_conv.shape[1]), F32)
        taps_grad_ref[...] = jnp.zeros_like(taps_grad_ref)
        wide_grad_ref[...] = jnp.zeros_like(wide_grad_ref)
        head_grad_ref[...] = jnp.zeros_like(head_grad_ref)

    grad = grad_ref[0]
    grad_hidden = [dot_nt(grad, out_own_ref[...]), dot_nt(grad, out_other_ref[...])]
    columns = jnp.concatenate([rows_ref[...], jnp.zeros((LANES - 8, CHUNK), F32)], axis=0).T
    scale = jnp.broadcast_to(columns[:, 0:1], (CHUNK, LANES))
    inner = jnp.broadcast_to(columns[:, 1:2], (CHUNK, LANES))
    for tile in range(width // LANES):
        lanes = slice(tile * LANES, (tile + 1) * LANES)
        at = tile * LANES % half
        back = grad_hidden[tile * LANES // half][:, at : at + LANES]
        gain = gain_ref[0:1, lanes]
        z = z_ref[0, :, lanes].astype(F32)
        gate = sigmoid(z)
        gated = z * gate
        y = y_ref[0, :, lanes].astype(F32)
        mixed = y * gated
        scaled_mixed = mixed * scale
        hidden_ref[0, :, lanes] = (scaled_mixed * gain).astype(BF16)
        wide_grad_ref[0:1, lanes] += jnp.sum(back * scaled_mixed, axis=0, keepdims=True)
        grad_mixed = scale * (back * gain) - mixed * inner
        dy = grad_mixed * gated
        grad_y[:, lanes] = dy
        grad_y_low[:, lanes] = dy.astype(BF16)
        dz = (grad_mixed * y * (gate + gated * (1.0 - gate))).astype(BF16)
        if tile * LANES < half:
            own_grad_ref[0, :, at : at + LANES] = dz
        else:
            other_grad_ref[0, :, at : at + LANES] = dz

    pre, step, log_decay, total, start, ending, kept = decays(
        raw_ref[0], head_ref, base, first_end, second_end, chunk
    )
    expander = head_expander(width)
    step_wide[...] = spread(step, expander)
    start_wide[...] = spread(start, expander)
    end_wide[...] = spread(ending, expander)
    kept_wide = spread(jnp.broadcast_to(kept, (8, LANES)), expander)[0:1]
    total_rows = total.T

    def activated(lanes):
        conv = conv_ref[0, :, lanes].astype(F32)
        gate = sigmoid(conv)
        value = conv * gate
        return value, gate + value * (1.0 - gate)

    b_lanes, c_lanes = slice(width, width + STATE), slice(width + STATE, width + 2 * STATE)
    b_f32, b_slope = activated(b_lanes)
    c_f32, c_slope = activated(c_lanes)
    b_low, c_low = b_f32.astype(BF16), c_f32.astype(BF16)
    state_low = state_ref[0]
    grad_state_low = grad_state[...].astype(BF16)
    from_state[...] = dot(c_low, state_low)
    to_state[...] = dot(b_low, grad_state_low)
    inter = dot_nt(b_low, c_low)

    def same_pairs(row_at, col_at):
        same, row_ids, col_ids = same_block(base + row_at, base + col_at, first_end, second_end)
        if row_at == col_at:
            same = same & (row_ids <= col_ids)
        return same

    same_00, same_01, same_11 = same_pairs(0, 0), same_pairs(0, HALF), same_pairs(HALF, HALF)
    inter_00 = jnp.where(same_00, inter[:HALF, :HALF], 0.0)
    inter_01 = jnp.where(same_01, inter[:HALF, HALF:], 0.0)
    inter_11 = jnp.where(same_11, inter[HALF:, HALF:], 0.0)
    low_lanes = iota((CHUNK, LANES), 1) < 64
    lane_ids = iota((CHUNK, LANES), 1)
    row_ids = iota((LANES, CHUNK), 0)
    col_sums = jnp.zeros((CHUNK, LANES), F32)
    row_sum_list = []
    grad_inter[...] = jnp.zeros_like(grad_inter)
    for tile in range(width // LANES):
        lanes = slice(tile * LANES, (tile + 1) * LANES)
        values, slope = activated(lanes)
        scaled = values * step_wide[:, lanes]
        scaled_low = scaled.astype(BF16)
        dy = grad_y[:, lanes]
        dy_low = grad_y_low[:, lanes]
        top, bottom = [], []
        for side_at in range(2):
            head = 2 * tile + side_at
            picked = low_lanes if side_at == 0 else ~low_lanes
            lhs = jnp.where(picked, scaled, 0.0).astype(BF16)
            pair_grad = dot_nt(lhs, dy_low)
            column = total[:, head : head + 1]
            row = total_rows[head : head + 1, :]
            top_col, low_col = column[:HALF], column[HALF:]
            top_row, low_row = row[:, :HALF], row[:, HALF:]
            decay_00 = jnp.exp2(jnp.minimum(top_row - top_col, 0.0))
            decay_01 = jnp.exp2(low_row - top_col)
            decay_11 = jnp.exp2(jnp.minimum(low_row - low_col, 0.0))
            part_00 = pair_grad[:HALF, :HALF] * decay_00
            part_01 = pair_grad[:HALF, HALF:] * decay_01
            part_11 = pair_grad[HALF:, HALF:] * decay_11
            grad_inter[:HALF, :HALF] += part_00
            grad_inter[:HALF, HALF:] += part_01
            grad_inter[HALF:, HALF:] += part_11
            full_00, full_01, full_11 = part_00 * inter_00, part_01 * inter_01, part_11 * inter_11
            top.append((inter_00 * decay_00).astype(BF16))
            top.append((inter_01 * decay_01).astype(BF16))
            bottom.append((inter_11 * decay_11).astype(BF16))
            col_sum = jnp.concatenate(
                [
                    jnp.sum(full_00 + full_01, axis=1, keepdims=True),
                    jnp.sum(full_11, axis=1, keepdims=True),
                ],
                axis=0,
            )
            col_sums = jnp.where(lane_ids == head, col_sum, col_sums)
            row_sum_list.append(
                jnp.concatenate(
                    [
                        jnp.sum(full_00, axis=0, keepdims=True),
                        jnp.sum(full_01 + full_11, axis=0, keepdims=True),
                    ],
                    axis=1,
                )
            )
        dy_parts = [
            jnp.where(low_lanes, dy, 0.0).astype(BF16),
            jnp.where(low_lanes, 0.0, dy).astype(BF16),
        ]
        local_top = dot(jnp.concatenate(top, axis=1), jnp.concatenate(dy_parts, axis=0))
        local_bottom = dot(
            jnp.concatenate(bottom, axis=1),
            jnp.concatenate([dy_parts[0][HALF:], dy_parts[1][HALF:]], axis=0),
        )
        local = jnp.concatenate([local_top, local_bottom], axis=0)
        tail = end_wide[:, lanes]
        back_state = to_state[:, lanes]
        grad_scaled = local + tail * back_state
        ended = scaled * tail
        end_x[:, lanes] = ended.astype(BF16)
        sum_end[:, lanes] = (ended * back_state).astype(BF16)
        started = dy * start_wide[:, lanes]
        start_dy[:, lanes] = started.astype(BF16)
        sum_start[:, lanes] = (started * from_state[:, lanes]).astype(BF16)
        sum_step[:, lanes] = (grad_scaled * values).astype(BF16)
        grad_values = step_wide[:, lanes] * grad_scaled + skip_ref[0:1, lanes] * dy
        wide_grad_ref[1:2, lanes] += jnp.sum(dy * values, axis=0, keepdims=True)
        grad_conv[:CHUNK, lanes] = grad_values * slope

    grad_inter_00 = jnp.where(same_00, grad_inter[:HALF, :HALF], 0.0)
    grad_inter_01 = jnp.where(same_01, grad_inter[:HALF, HALF:], 0.0)
    grad_inter_11 = jnp.where(same_11, grad_inter[HALF:, HALF:], 0.0)
    pair_t = jnp.concatenate(
        [
            jnp.concatenate([grad_inter_00, grad_inter_01], axis=1),
            jnp.concatenate([jnp.zeros((HALF, HALF), F32), grad_inter_11], axis=1),
        ],
        axis=0,
    )
    grad_b = dot(pair_t.astype(BF16), c_low) + dot_nt(end_x[...], grad_state_low)
    grad_c = dot(pair_t.T.astype(BF16), b_low) + dot_nt(start_dy[...], state_low)
    grad_conv[:CHUNK, b_lanes] = grad_b * b_slope
    grad_conv[:CHUNK, c_lanes] = grad_c * c_slope

    folder = head_folder(width)
    end_sums = dot(sum_end[...], folder)
    start_sums = dot(sum_start[...], folder)
    step_sums = dot(sum_step[...], folder)
    state_pairs = jnp.sum(grad_state[...] * state_low.astype(F32), axis=0, keepdims=True)
    first, second = pieces(jnp.broadcast_to(state_pairs, (8, width)), 2)
    state_sums = (dot(first, folder) + dot(second, folder))[0:1] * kept
    row_sums = jnp.concatenate(
        row_sum_list + [jnp.zeros((LANES - len(row_sum_list), CHUNK), F32)], axis=0
    ).T
    grad_total = row_sums - col_sums + start_sums - end_sums
    last = state_sums + jnp.sum(end_sums, axis=0, keepdims=True)
    grad_total = grad_total + jnp.where(iota((CHUNK, LANES), 0) == CHUNK - 1, last, 0.0)
    grad_decay = dot_exact(upper_ones(), grad_total)
    grad_step = step_sums - grad_decay * head_ref[1:2, :]
    grad_raw = grad_step * sigmoid(pre)
    head_grad_ref[0:1, :] += jnp.sum(grad_raw, axis=0, keepdims=True)
    head_grad_ref[1:2, :] += jnp.sum(grad_decay * log_decay, axis=0, keepdims=True)
    step_grad_ref[0] = grad_raw.astype(BF16)
    grad_state[...] = kept_wide * grad_state[...] + dot(c_f32.T.astype(BF16), start_dy[...])

    rows = base + iota((CHUNK, LANES), 0)
    segment = segment_of(rows, first_end, second_end)
    masks = [
        (segment_of(rows + lag, first_end, second_end) == segment).astype(F32)
        for lag in range(1, 4)
    ]
    for tile in range((width + 2 * STATE) // LANES):
        lanes = slice(tile * LANES, (tile + 1) * LANES)
        inputs = input_ref[0, :, lanes].astype(F32)
        current = grad_conv[:CHUNK, lanes]
        found = taps_ref[3:4, lanes] * current
        taps_grad_ref[4:5, lanes] += jnp.sum(current, axis=0, keepdims=True)
        taps_grad_ref[3:4, lanes] += jnp.sum(current * inputs, axis=0, keepdims=True)
        for lag in range(1, 4):
            shifted = grad_conv[lag : lag + CHUNK, lanes] * masks[lag - 1]
            found = found + taps_ref[3 - lag : 4 - lag, lanes] * shifted
            taps_grad_ref[3 - lag : 4 - lag, lanes] += jnp.sum(
                shifted * inputs, axis=0, keepdims=True
            )
        found = found.astype(BF16)
        if tile * LANES < half:
            own_grad_ref[0, :, half + tile * LANES : half + (tile + 1) * LANES] = found
        elif tile * LANES < width:
            other_grad_ref[0, :, tile * LANES : (tile + 1) * LANES] = found
        elif tile * LANES == width:
            shared_b = found
        else:
            own_grad_ref[0, :, width:] = jnp.where(side == 0, shared_b, found)
            other_grad_ref[0, :, width:] = jnp.where(side == 0, found, shared_b)
    grad_conv[CHUNK:, :] = grad_conv[0:8, :]
    back_ref[0] = (
        dot_nt(own_grad_ref[0], own_ref[...])
        + dot_nt(other_grad_ref[0], other_ref[...])
        + dot_nt(step_grad_ref[0], step_ref[...])
    ).astype(BF16)


def whole(shape):
    return pl.BlockSpec(shape, lambda i, s: (0,) * len(shape))


def run_forward(scalars, slots, weights, grad_slots):
    own, other, step, out_own, out_other, taps, gain, skip, head = weights
    count, rows, depth = slots.shape
    width = gain.shape[1]
    joined = width + 2 * STATE

    def slot(cols, height=rows):
        return pl.BlockSpec((1, height, cols), lambda i, s: (i ^ s[3], 0, 0))

    inputs = [slots, own, other, step, out_own, out_other, taps, gain, skip, head]
    in_specs = [slot(depth)] + [whole(a.shape) for a in inputs[1:]]
    if grad_slots is not None:
        inputs.append(grad_slots)
        in_specs.append(slot(depth))
    return pl.pallas_call(
        forward_kernel,
        grid_spec=pltpu.PrefetchScalarGridSpec(
            num_scalar_prefetch=1,
            grid=(count,),
            in_specs=in_specs,
            out_specs=[
                slot(depth),
                pl.BlockSpec((8, CHUNK), lambda i, s: (0, i)),
                slot(width),
                slot(joined),
                slot(joined),
                slot(width),
                slot(LANES),
                slot(width, STATE),
            ],
            scratch_shapes=[
                pltpu.VMEM((CHUNK + 8, joined), F32),
                pltpu.VMEM((STATE, width), F32),
                pltpu.VMEM((CHUNK, width), BF16),
                pltpu.VMEM((CHUNK, width), BF16),
            ]
            + [pltpu.VMEM((CHUNK, width), F32)] * 4,
        ),
        out_shape=[
            jax.ShapeDtypeStruct((count, rows, depth), BF16),
            jax.ShapeDtypeStruct((8, count * rows), F32),
            jax.ShapeDtypeStruct((count, rows, width), BF16),
            jax.ShapeDtypeStruct((count, rows, joined), BF16),
            jax.ShapeDtypeStruct((count, rows, joined), BF16),
            jax.ShapeDtypeStruct((count, rows, width), BF16),
            jax.ShapeDtypeStruct((count, rows, LANES), F32),
            jax.ShapeDtypeStruct((count, STATE, width), BF16),
        ],
        compiler_params=pltpu.CompilerParams(vmem_limit_bytes=VMEM_LIMIT),
        name="forward_mixer",
    )(scalars, *inputs)


def run_backward(scalars, grad_slots, row_values, weights, kept):
    own, other, step, out_own, out_other, taps, gain, skip, head = weights
    count, rows, depth = grad_slots.shape
    width = gain.shape[1]
    joined = width + 2 * STATE
    final = count - 1

    def slot(cols, height=rows):
        return pl.BlockSpec((1, height, cols), lambda i, s: ((final - i) ^ s[3], 0, 0))

    z, conv, inputs, y, raw, states = kept
    constants = [own, other, step, out_own, out_other, taps, gain, skip, head]
    return pl.pallas_call(
        backward_kernel,
        grid_spec=pltpu.PrefetchScalarGridSpec(
            num_scalar_prefetch=1,
            grid=(count,),
            in_specs=[slot(depth), pl.BlockSpec((8, CHUNK), lambda i, s: (0, final - i))]
            + [whole(a.shape) for a in constants]
            + [slot(width), slot(joined), slot(joined), slot(width), slot(LANES)]
            + [slot(width, STATE)],
            out_specs=[
                slot(depth),
                slot(own.shape[1]),
                slot(own.shape[1]),
                slot(LANES),
                slot(width),
                whole((8, joined)),
                whole((8, width)),
                whole((8, LANES)),
            ],
            scratch_shapes=[
                pltpu.VMEM((STATE, width), F32),
                pltpu.VMEM((CHUNK + 8, joined), F32),
                pltpu.VMEM((CHUNK, width), F32),
                pltpu.VMEM((CHUNK, width), BF16),
            ]
            + [pltpu.VMEM((CHUNK, width), F32)] * 5
            + [pltpu.VMEM((CHUNK, width), BF16)] * 5
            + [pltpu.VMEM((CHUNK, CHUNK), F32)],
        ),
        out_shape=[
            jax.ShapeDtypeStruct((count, rows, depth), BF16),
            jax.ShapeDtypeStruct((count, rows, own.shape[1]), BF16),
            jax.ShapeDtypeStruct((count, rows, own.shape[1]), BF16),
            jax.ShapeDtypeStruct((count, rows, LANES), BF16),
            jax.ShapeDtypeStruct((count, rows, width), BF16),
            jax.ShapeDtypeStruct((8, joined), F32),
            jax.ShapeDtypeStruct((8, width), F32),
            jax.ShapeDtypeStruct((8, LANES), F32),
        ],
        compiler_params=pltpu.CompilerParams(vmem_limit_bytes=VMEM_LIMIT),
        name="backward_mixer",
    )(scalars, grad_slots, row_values, *constants, z, conv, inputs, y, raw, states)


def crossing(bit):
    return [(i, i ^ bit) for i in range(4)]


def exchange(block, bit):
    return lax.ppermute(block, "tensor", crossing(bit))


def swap_cores(block):
    return lax.ppermute(block, "pipe", [(0, 1), (1, 0)])


def gather_rows(block):
    cols = block.shape[1] // 2
    left, right = block[:, :cols], block[:, cols:]
    left_1 = exchange(left, 1)
    right_2 = exchange(right, 2)
    left_23 = exchange(jnp.stack([left, left_1]), 2)
    right_13 = exchange(jnp.stack([right, right_2]), 1)
    return jnp.stack(
        [
            block,
            jnp.concatenate([left_1, right_13[0]], axis=1),
            jnp.concatenate([left_23[0], right_2], axis=1),
            jnp.concatenate([left_23[1], right_13[1]], axis=1),
        ]
    )


def scatter_rows(slots):
    cols = slots.shape[2] // 2
    left, right = slots[:, :, :cols], slots[:, :, cols:]
    got_left = exchange(left[2:], 2)
    got_right = exchange(jnp.stack([right[1], right[3]]), 1)
    left_0 = left[0].astype(F32) + got_left[0].astype(F32)
    left_1 = left[1].astype(F32) + got_left[1].astype(F32)
    right_0 = right[0].astype(F32) + got_right[0].astype(F32)
    right_2 = right[2].astype(F32) + got_right[1].astype(F32)
    last_left = exchange(left_1.astype(BF16), 1)
    last_right = exchange(right_2.astype(BF16), 2)
    return jnp.concatenate(
        [left_0 + last_left.astype(F32), right_0 + last_right.astype(F32)], axis=1
    )


def sum_tensor(value):
    value = value + exchange(value, 1)
    return value + exchange(value, 2)


def rms_scale(x):
    return lax.rsqrt(jnp.mean(x * x, axis=1, keepdims=True) + NORM_EPSILON)


def shards(
    tokens,
    out_grad,
    seq_lengths,
    norm_gain,
    w_zx,
    w_bc,
    w_dt,
    conv_x,
    conv_bc,
    out_gain,
    head_params,
    out_weight,
):
    core = lax.axis_index("pipe")
    place = lax.axis_index("tensor")
    is_first = core == 0
    fsdp_count = lax.axis_size("fsdp")
    local_depth = norm_gain.shape[1]
    depth = local_depth * fsdp_count
    width = w_zx.shape[3]
    half = width // 2
    head_count = w_dt.shape[2]
    head_size = width // head_count
    local_head = conv_x.shape[3]
    inner_total = width * lax.axis_size("tensor")
    local_rows = tokens.shape[1]
    joined = width + 2 * STATE
    tap_rows = conv_x.shape[1]

    def by_core(first, second):
        return jnp.where(is_first, first, second)

    def local_order(value):
        size = value.shape[-1] // 2
        return by_core(
            value, jnp.concatenate([value[..., size:], value[..., :size]], axis=-1)
        )

    x_0 = lax.dynamic_index_in_dim(tokens, core, 0, keepdims=False).astype(F32)
    cotangent = lax.dynamic_index_in_dim(out_grad, core, 0, keepdims=False)
    lengths = lax.dynamic_index_in_dim(seq_lengths, core, 0, keepdims=False)[0]
    scalars = jnp.stack([core, lengths[0], lengths[0] + lengths[1], place]).astype(jnp.int32)

    def halves(which):
        at = which * half
        return jnp.concatenate(
            [
                lax.dynamic_slice_in_dim(w_zx[0, :, 0], at, half, 1),
                lax.dynamic_slice_in_dim(w_zx[0, :, 1], at, half, 1),
                lax.dynamic_slice_in_dim(w_bc[0], which * STATE, STATE, 1),
            ],
            axis=1,
        )

    mine, theirs = halves(core), swap_cores(halves(1 - core))
    mine_out = lax.dynamic_slice_in_dim(out_weight[0], core * half, half, 0)
    theirs_out = swap_cores(lax.dynamic_slice_in_dim(out_weight[0], (1 - core) * half, half, 0))

    small = [norm_gain[0], w_dt[0], conv_x[0], conv_bc[0], out_gain[0]]
    packed = jnp.concatenate([a.reshape(-1) for a in small])
    small_size = packed.shape[0]
    packed = jnp.pad(packed, (0, -small_size % 2048)).reshape(16, -1)
    small_own = lax.all_gather(packed, "fsdp", axis=0, tiled=False)
    small_swapped = swap_cores(small_own)
    heads_own = jnp.pad(head_params[0], ((0, 5), (0, LANES - head_count)))
    heads_swapped = swap_cores(heads_own)

    def section_weights(section):
        def pick(own, swapped):
            return by_core(own, swapped) if section == 0 else by_core(swapped, own)

        flat = pick(small_own, small_swapped).reshape(fsdp_count, -1)
        at = 0
        arrays = []
        for array in small:
            arrays.append(flat[:, at : at + array.size].reshape((fsdp_count,) + array.shape))
            at += array.size
        gain_parts, step_parts, conv_parts, shared_parts, scale_parts = arrays
        gain_vec = gain_parts.reshape(1, depth).astype(F32)
        step_full = jnp.pad(
            local_order(step_parts.reshape(depth, head_count)),
            ((0, 0), (0, LANES - head_count)),
        )
        conv_full = local_order(
            jnp.moveaxis(conv_parts, 0, 2).reshape(tap_rows, width).astype(F32)
        )
        shared_full = jnp.moveaxis(shared_parts, 0, 1).reshape(tap_rows, 2 * STATE).astype(F32)
        taps = jnp.pad(
            jnp.concatenate([conv_full, shared_full], axis=1), ((0, 8 - tap_rows), (0, 0))
        )
        scale = local_order(jnp.moveaxis(scale_parts, 0, 1).reshape(1, width).astype(F32))
        heads = pick(heads_own, heads_swapped)[:3, :head_count]
        heads = local_order(heads)
        skip = jnp.repeat(heads[2], head_size).reshape(1, width)
        head_rows = jnp.pad(
            jnp.stack([heads[0], jnp.exp(heads[1])]), ((0, 6), (0, LANES - head_count))
        )
        own = lax.all_gather(pick(mine, theirs), "fsdp", axis=0, tiled=True)
        out_own = lax.all_gather(pick(mine_out, theirs_out), "fsdp", axis=1, tiled=True)
        other = swap_cores(own)
        out_other = swap_cores(out_own)
        return gain_vec, (own, other, step_full, out_own, out_other, taps, scale, skip, head_rows)

    sections = [section_weights(0), section_weights(1)]

    cotangent_slots = gather_rows(cotangent)

    x = x_0
    saved = []
    results = []
    for section in range(2):
        gain_vec, weights = sections[section]
        normed = (x * rms_scale(x) * gain_vec).astype(BF16)
        slots = gather_rows(normed)
        part, sums, *kept = run_forward(
            scalars, slots, weights, cotangent_slots if section == 1 else None
        )
        sums = sum_tensor(sums[:2])
        scale_rows = lax.rsqrt(sums[0] / inner_total + NORM_EPSILON)
        own_scale = lax.dynamic_slice_in_dim(scale_rows, place * local_rows, local_rows, 0)
        summed = scatter_rows(part)
        y = x + summed * own_scale[:, None]
        saved.append((x, slots, kept, scale_rows, sums[1], summed))
        x_low = y.astype(BF16)
        results.append(x_low)
        x = x_low.astype(F32)

    def add_cores(own_part, other_part):
        got = swap_cores(other_part.astype(BF16))
        return (own_part + got.astype(F32)).astype(BF16)

    grad_low = cotangent
    grad_slots = cotangent_slots
    grads_x = [None, None]
    reduced = [None, None]
    for section in (1, 0):
        gain_vec, weights = sections[section]
        x, slots, kept, scale_rows, crossed, summed = saved[section]
        if section == 0:
            grad_slots = gather_rows(grad_low)
            own_cross = jnp.sum(grad_low.astype(F32) * summed, axis=1)
            crossed = lax.all_gather(own_cross, "tensor", axis=0, tiled=True)
        inner = scale_rows * scale_rows * scale_rows * crossed / inner_total
        row_values = jnp.pad(jnp.stack([scale_rows, inner]), ((0, 6), (0, 0)))
        back, own_grad, other_grad, step_grad, hidden, taps_grad, wide_grad, head_grad = (
            run_backward(scalars, grad_slots, row_values, weights, kept)
        )
        dnormed = scatter_rows(back)
        scale = rms_scale(x)
        weighted = dnormed * gain_vec
        dx = (
            grad_low.astype(F32)
            + weighted * scale
            - x * (scale * scale * scale * jnp.mean(weighted * x, axis=1, keepdims=True))
        )
        gain_grad = jnp.sum(dnormed * (x * scale), axis=0)
        all_rows = slots.shape[0] * slots.shape[1]
        flat_slots = slots.reshape(all_rows, depth)
        flat_grads = grad_slots.reshape(all_rows, depth)
        flat_hidden = hidden.reshape(all_rows, width)
        out_sum = add_cores(
            dot_tn(flat_hidden[:, :half], flat_grads), dot_tn(flat_hidden[:, half:], flat_grads)
        )
        out_reduced = lax.psum_scatter(out_sum, "fsdp", scatter_dimension=1, tiled=True)
        in_sum = add_cores(
            dot_tn(flat_slots, own_grad.reshape(all_rows, -1)),
            dot_tn(flat_slots, other_grad.reshape(all_rows, -1)),
        )
        in_reduced = lax.psum_scatter(in_sum, "fsdp", scatter_dimension=0, tiled=True)
        step_sum = local_order(
            dot_tn(flat_slots, step_grad.reshape(all_rows, LANES))[:, :head_count]
        )
        head_sum = local_order(
            jnp.concatenate(
                [
                    head_grad[:2, :head_count],
                    jnp.sum(wide_grad[1].reshape(head_count, head_size), axis=1)[None],
                ]
            )
        )
        split_small = [
            step_sum,
            local_order(taps_grad[:tap_rows, :width]),
            local_order(wide_grad[0:1]),
            head_sum,
        ]
        shared_small = [gain_grad, taps_grad[:tap_rows, width:]]
        split_sum = lax.psum(
            jnp.concatenate([a.reshape(-1) for a in split_small]), ("pipe", "fsdp")
        )
        shared_sum = lax.psum(
            jnp.concatenate([a.reshape(-1) for a in shared_small]), ("pipe", "fsdp", "tensor")
        )
        reduced[section] = (out_reduced, in_reduced, split_sum, shared_sum)
        grad_low = dx.astype(BF16)
        grads_x[section] = grad_low

    def both_micros(first, second):
        keep, send = by_core(first, second), by_core(second, first)
        got = swap_cores(send)
        return jnp.stack([by_core(keep, got), by_core(got, keep)])[None]

    section_out = both_micros(results[0], results[1])
    input_out = both_micros(grads_x[0], grads_x[1])

    def both_halves(first, second):
        keep, send = by_core(first, second), by_core(second, first)
        got = swap_cores(send)
        return by_core(keep, got), by_core(got, keep)

    out_low, out_high = both_halves(reduced[0][0], reduced[1][0])
    grad_out_weight = jnp.concatenate([out_low, out_high], axis=0).astype(F32)
    in_low, in_high = both_halves(reduced[0][1], reduced[1][1])
    grad_zx = jnp.stack(
        [
            jnp.concatenate([in_low[:, :half], in_high[:, :half]], axis=1),
            jnp.concatenate([in_low[:, half:width], in_high[:, half:width]], axis=1),
        ],
        axis=1,
    ).astype(F32)
    grad_bc = lax.psum_scatter(
        jnp.concatenate([in_low[:, width:], in_high[:, width:]], axis=1).astype(F32),
        "tensor",
        scatter_dimension=0,
        tiled=True,
    )
    flat = by_core(reduced[0][2], reduced[1][2])
    sizes = [depth * head_count, tap_rows * width, width]
    fsdp_at = lax.axis_index("fsdp")
    grad_dt = lax.dynamic_slice_in_dim(
        flat[: sizes[0]].reshape(depth, head_count), fsdp_at * local_depth, local_depth, 0
    )
    at = sizes[0]
    grad_conv = lax.dynamic_slice_in_dim(
        flat[at : at + sizes[1]].reshape(tap_rows, head_count, head_size),
        fsdp_at * local_head,
        local_head,
        2,
    )
    at += sizes[1]
    grad_scale = lax.dynamic_slice_in_dim(
        flat[at : at + sizes[2]].reshape(head_count, head_size),
        fsdp_at * local_head,
        local_head,
        1,
    )
    at += sizes[2]
    grad_heads = flat[at:].reshape(3, head_count)
    flat = by_core(reduced[0][3], reduced[1][3])
    all_at = fsdp_at * lax.axis_size("tensor") + place
    piece = depth // (fsdp_count * lax.axis_size("tensor"))
    grad_gain = lax.dynamic_slice_in_dim(flat[:depth], all_at * piece, piece, 0)
    piece = 2 * STATE // (fsdp_count * lax.axis_size("tensor"))
    grad_shared = lax.dynamic_slice_in_dim(
        flat[depth:].reshape(tap_rows, 2 * STATE), all_at * piece, piece, 1
    )
    return (
        section_out,
        input_out,
        grad_gain[None],
        grad_zx[None],
        grad_bc[None],
        grad_dt[None],
        grad_conv[None],
        grad_shared[None],
        grad_scale[None],
        grad_heads[None],
        grad_out_weight[None],
    )


def solution(mesh):
    return jax.shard_map(
        shards,
        mesh=mesh,
        in_specs=(
            P(None, ("fsdp", "tensor"), None),
            P(None, ("fsdp", "tensor"), None),
            P(None, "fsdp", None),
            P("pipe", "fsdp"),
            P("pipe", "fsdp", None, "tensor"),
            P("pipe", "fsdp", None),
            P("pipe", "fsdp", "tensor"),
            P("pipe", None, "tensor", "fsdp"),
            P("pipe", None, "fsdp"),
            P("pipe", "tensor", "fsdp"),
            P("pipe", None, "tensor"),
            P("pipe", "tensor", "fsdp"),
        ),
        out_specs=(
            P("pipe", None, ("fsdp", "tensor"), None),
            P("pipe", None, ("fsdp", "tensor"), None),
            P("pipe", ("fsdp", "tensor")),
            P("pipe", "fsdp", None, "tensor"),
            P("pipe", ("fsdp", "tensor"), None),
            P("pipe", "fsdp", "tensor"),
            P("pipe", None, "tensor", "fsdp"),
            P("pipe", None, ("fsdp", "tensor")),
            P("pipe", "tensor", "fsdp"),
            P("pipe", None, "tensor"),
            P("pipe", "tensor", "fsdp"),
        ),
        check_vma=False,
    )
```

```python
import functools

import jax
import jax.numpy as jnp
import numpy as np
from jax import lax
from jax.experimental import pallas as pl
from jax.experimental.pallas import tpu as pltpu
from jax.sharding import PartitionSpec as P

STATE = 128
CHUNK = 256
EXTRA = 16
HALF = 128
LANES = 128
NORM_EPSILON = 1e-05
LOG2E = 1.4426950408889634
F32 = jnp.float32
BF16 = jnp.bfloat16
VMEM_LIMIT = 56 * 1024 * 1024


def dot(a, b):
    return lax.dot_general(a, b, (((1,), (0,)), ((), ())), preferred_element_type=F32)


def dot_nt(a, b):
    return lax.dot_general(a, b, (((1,), (1,)), ((), ())), preferred_element_type=F32)


def dot_tn(a, b):
    return lax.dot_general(a, b, (((0,), (0,)), ((), ())), preferred_element_type=F32)


def pieces(value, count):
    found = []
    for _ in range(count):
        part = value.astype(BF16)
        found.append(part)
        value = value - part.astype(F32)
    return found


def dot_exact(ones, value):
    first, second, third = pieces(value, 3)
    return dot(ones, first) + (dot(ones, second) + dot(ones, third))


def spread(value, expander):
    first, second = pieces(value, 2)
    return dot(first, expander) + dot(second, expander)


def sigmoid(value):
    return 0.5 * jnp.tanh(0.5 * value) + 0.5


def softplus(value):
    return jnp.maximum(value, 0.0) + jnp.log1p(jnp.exp(-jnp.abs(value)))


def iota(shape, axis):
    return lax.broadcasted_iota(jnp.int32, shape, axis)


def segment_of(rows, first_end, second_end):
    return (rows >= first_end).astype(jnp.int32) + (rows >= second_end).astype(jnp.int32)


def head_expander(width):
    size = (LANES, width)
    return (iota(size, 0) == iota(size, 1) // 64).astype(BF16)


def head_folder(width):
    size = (width, LANES)
    return (iota(size, 1) == iota(size, 0) // 64).astype(BF16)


def lower_ones():
    size = (CHUNK, CHUNK)
    return (iota(size, 0) >= iota(size, 1)).astype(BF16)


def upper_ones():
    size = (CHUNK, CHUNK)
    return (iota(size, 0) <= iota(size, 1)).astype(BF16)


def decays(raw, head_ref, base, first_end, second_end, chunk):
    pre = raw + head_ref[0:1, :]
    step = softplus(pre)
    log_decay = -step * jnp.exp(head_ref[1:2, :])
    total = dot_exact(lower_ones(), log_decay) * LOG2E
    rows = base + iota((CHUNK, LANES), 0)
    segment = segment_of(rows, first_end, second_end)
    previous = jnp.where(chunk == 0, -1, segment_of(base - 1, first_end, second_end))
    final = segment_of(base + CHUNK - 1, first_end, second_end)
    last = total[CHUNK - 1 : CHUNK, :]
    start = jnp.where(segment == previous, jnp.exp2(total), 0.0)
    ending = jnp.where(segment == final, jnp.exp2(last - total), 0.0)
    kept = jnp.where(final == previous, jnp.exp2(last), 0.0)
    return pre, step, log_decay, total, start, ending, kept


def same_block(row_base, col_base, first_end, second_end):
    size = (HALF, HALF)
    rows = row_base + iota(size, 0)
    cols = col_base + iota(size, 1)
    return (
        (segment_of(rows, first_end, second_end) == segment_of(cols, first_end, second_end)),
        rows,
        cols,
    )


def pick_rows(target, blocks, slot, extra=None):
    rows, cols = target.shape[0], target.shape[1] // 2
    for at in range(3):

        @pl.when(slot == at)
        def _():
            target[...] = blocks[at][:rows, :]
            if extra is not None:
                extra[...] = blocks[at][rows:, :cols]

    @pl.when(slot == 3)
    def _():
        target[:, :cols] = blocks[3][:rows, :]
        target[:, cols:] = blocks[4][:rows, :]
        if extra is not None:
            extra[...] = blocks[3][rows:, :]


def put_rows(targets, value, slot):
    parts = len(targets) // 4
    cols = value.shape[1] // parts
    for at in range(4):

        @pl.when(slot == at)
        def _():
            for part in range(parts):
                targets[4 * part + at][...] = value[:, part * cols : (part + 1) * cols].astype(
                    BF16
                )


def normalise(x_rows, norm_ref):
    depth = x_rows.shape[1]
    squares = jnp.zeros((CHUNK, LANES), F32)
    for tile in range(depth // LANES):
        lanes = slice(tile * LANES, (tile + 1) * LANES)
        x = x_rows[:, lanes].astype(F32)
        squares = squares + x * x
    scale = lax.rsqrt(jnp.sum(squares, axis=1, keepdims=True) / depth + NORM_EPSILON)
    scale = jnp.broadcast_to(scale, (CHUNK, LANES))
    for tile in range(depth // LANES):
        lanes = slice(tile * LANES, (tile + 1) * LANES)
        x = x_rows[:, lanes].astype(F32)
        x_rows[:, lanes] = (x * scale * norm_ref[0:1, lanes]).astype(BF16)


def padded_step(step_ref):
    rows, cols = step_ref.shape
    return jnp.concatenate([step_ref[...], jnp.zeros((LANES - rows, cols), BF16)], axis=0)


def mixer_kernel(scalars, *refs):
    blocks = refs[:5]
    (
        own_ref,
        other_ref,
        step_ref,
        norm_ref,
        taps_ref,
        head_ref,
        slots_ref,
        conv_ref,
        input_ref,
        y_ref,
        raw_ref,
        state_ref,
        x_rows,
        joined,
        state,
        end_x,
        from_state,
        step_wide,
        start_wide,
        end_wide,
    ) = refs[5:]
    chunk = pl.program_id(0)
    side, first_end, second_end = scalars[0], scalars[1], scalars[2]
    base = chunk * CHUNK
    width = end_x.shape[1]
    half = width // 2

    @pl.when(chunk == 0)
    def _():
        state[...] = jnp.zeros_like(state)
        joined[0:8, :] = jnp.zeros((8, joined.shape[1]), F32)

    pick_rows(x_rows, blocks, chunk ^ scalars[3])
    normalise(x_rows, norm_ref)
    x = x_rows[...]
    slots_ref[0] = x
    shared = half + STATE
    own = dot(x, own_ref[:, :shared])
    other = dot(x, other_ref[:, :shared])
    raw = dot_nt(x, padded_step(step_ref))
    raw_ref[0] = raw
    joined[8:, :half] = own[:, :half]
    joined[8:, half:width] = other[:, :half]
    joined[8:, width : width + STATE] = jnp.where(side == 0, own[:, half:], other[:, half:])
    joined[8:, width + STATE :] = jnp.where(side == 0, other[:, half:], own[:, half:])

    _, step, _, total, start, ending, kept = decays(
        raw, head_ref, base, first_end, second_end, chunk
    )
    expander = head_expander(width)
    step_wide[...] = spread(step, expander)
    start_wide[...] = spread(start, expander)
    end_wide[...] = spread(ending, expander)
    kept_wide = spread(jnp.broadcast_to(kept, (8, LANES)), expander)[0:1]
    skip = spread(jnp.broadcast_to(head_ref[2:3, :], (8, LANES)), expander)[0:1]
    total_rows = total.T

    rows = base + iota((CHUNK, LANES), 0)
    inside = rows - jnp.where(
        rows >= second_end, second_end, jnp.where(rows >= first_end, first_end, 0)
    )
    masks = [(inside >= lag).astype(F32) for lag in range(1, 4)]

    def activate(lanes):
        current = joined[8:, lanes]
        found = taps_ref[4:5, lanes] + taps_ref[3:4, lanes] * current
        for lag in range(1, 4):
            shifted = joined[8 - lag : 8 - lag + CHUNK, lanes] * masks[lag - 1]
            found = found + taps_ref[3 - lag : 4 - lag, lanes] * shifted
        conv_ref[0, :, lanes] = found.astype(BF16)
        input_ref[0, :, lanes] = current.astype(BF16)
        return found * sigmoid(found)

    b_f32 = activate(slice(width, width + STATE))
    b_low = b_f32.astype(BF16)
    c_low = activate(slice(width + STATE, width + 2 * STATE)).astype(BF16)
    state_ref[0] = state[...].astype(BF16)
    from_state[...] = dot(c_low, state[...].astype(BF16))
    inter = dot_nt(c_low, b_low)

    def masked(row_at, col_at):
        same, row_ids, col_ids = same_block(base + row_at, base + col_at, first_end, second_end)
        if row_at == col_at:
            same = same & (row_ids >= col_ids)
        return jnp.where(same, inter[row_at : row_at + HALF, col_at : col_at + HALF], 0.0)

    inter_00, inter_10, inter_11 = masked(0, 0), masked(HALF, 0), masked(HALF, HALF)
    low_lanes = iota((CHUNK, LANES), 1) < 64
    for tile in range(width // LANES):
        lanes = slice(tile * LANES, (tile + 1) * LANES)
        values = activate(lanes)
        scaled = values * step_wide[:, lanes]
        end_x[:, lanes] = (scaled * end_wide[:, lanes]).astype(BF16)
        scaled_parts = [
            jnp.where(low_lanes, scaled, 0.0).astype(BF16),
            jnp.where(low_lanes, 0.0, scaled).astype(BF16),
        ]
        top, bottom = [], []
        for side_at in range(2):
            head = 2 * tile + side_at
            column = total[:, head : head + 1]
            row = total_rows[head : head + 1, :]
            top_col, low_col = column[:HALF], column[HALF:]
            top_row, low_row = row[:, :HALF], row[:, HALF:]
            top.append((inter_00 * jnp.exp2(jnp.minimum(top_col - top_row, 0.0))).astype(BF16))
            bottom.append((inter_10 * jnp.exp2(low_col - top_row)).astype(BF16))
            bottom.append((inter_11 * jnp.exp2(jnp.minimum(low_col - low_row, 0.0))).astype(BF16))
        local_top = dot(
            jnp.concatenate(top, axis=1),
            jnp.concatenate([scaled_parts[0][:HALF], scaled_parts[1][:HALF]], axis=0),
        )
        local_bottom = dot(
            jnp.concatenate(bottom, axis=1), jnp.concatenate(scaled_parts, axis=0)
        )
        local = jnp.concatenate([local_top, local_bottom], axis=0)
        y = local + from_state[:, lanes] * start_wide[:, lanes] + skip[:, lanes] * values
        y_ref[0, :, lanes] = y.astype(BF16)
    state[...] = kept_wide * state[...] + dot(b_f32.T.astype(BF16), end_x[...])
    joined[0:8, :] = joined[CHUNK : CHUNK + 8, :]


def gate_kernel(scalars, x_ref, own_ref, other_ref, gain_ref, y_ref, *rest):
    z_ref, hidden_ref, sums_ref = rest
    width = hidden_ref.shape[2]
    half = width // 2
    x = x_ref[0]
    offset = own_ref.shape[1] - half
    gates = [dot(x, own_ref[:, offset:]), dot(x, other_ref[:, offset:])]
    squares = jnp.zeros((CHUNK, LANES), F32)
    for tile in range(width // LANES):
        lanes = slice(tile * LANES, (tile + 1) * LANES)
        at = tile * LANES % half
        z = gates[tile * LANES // half][:, at : at + LANES]
        z_ref[0, :, lanes] = z.astype(BF16)
        mixed = y_ref[0, :, lanes].astype(F32) * (z * sigmoid(z))
        squares = squares + mixed * mixed
        hidden_ref[0, :, lanes] = (mixed * gain_ref[5:6, lanes]).astype(BF16)
    ones = jnp.ones((8, LANES), BF16)
    first, second = pieces(squares, 2)
    sums_ref[...] = dot_nt(ones, first) + dot_nt(ones, second)


def project_kernel(scalars, hidden_ref, own_ref, other_ref, *out_refs):
    hidden = hidden_ref[0]
    half = hidden.shape[1] // 2
    found = dot(hidden[:, :half], own_ref[...]) + dot(hidden[:, half:], other_ref[...])
    if len(out_refs) == 8:
        put_rows(out_refs, found, pl.program_id(0))
    else:
        grad_ref, *out_refs, sums_ref = out_refs
        put_rows(out_refs, found, pl.program_id(0))
        crossed = jnp.zeros((CHUNK, LANES), F32)
        for tile in range(found.shape[1] // LANES):
            lanes = slice(tile * LANES, (tile + 1) * LANES)
            crossed = crossed + found[:, lanes] * grad_ref[0, :, lanes].astype(F32)
        ones = jnp.ones((8, LANES), BF16)
        first, second = pieces(crossed, 2)
        sums_ref[...] = dot_nt(ones, first) + dot_nt(ones, second)


def gate_backward_kernel(inner_factor, scalars, *refs):
    early = len(refs) < 15
    if early:
        back_refs, refs = refs[:2], refs[2:]
        backs = [ref[0].astype(F32) for ref in back_refs]
    else:
        blocks, (out_own_ref, out_other_ref), refs = refs[:5], refs[5:7], refs[7:]
        refs, (natural_ref, grad_rows, extra) = refs[:-3], refs[-3:]
        pick_rows(grad_rows, blocks, pl.program_id(0), extra)
        grad = grad_rows[...]
        natural_ref[0] = grad
        backs = [dot_nt(grad, out_own_ref[...]), dot_nt(grad, out_other_ref[...])]
    (
        rows_ref,
        gain_ref,
        z_ref,
        y_ref,
        own_grad_ref,
        other_grad_ref,
        hidden_ref,
        grad_y_ref,
        gain_grad_ref,
    ) = refs
    width = hidden_ref.shape[2]
    half = width // 2

    @pl.when(pl.program_id(0) == 0)
    def _():
        gain_grad_ref[...] = jnp.zeros_like(gain_grad_ref)

    scale_row = rows_ref[0:1, :]
    if early:
        crossed = rows_ref[1:2, :]
    else:
        parts = extra[0:1, : 3 * CHUNK].astype(F32)
        crossed = parts[:, :CHUNK] + (parts[:, CHUNK : 2 * CHUNK] + parts[:, 2 * CHUNK :])
    inner_row = scale_row * scale_row * scale_row * crossed * inner_factor
    columns = jnp.concatenate(
        [scale_row, inner_row, jnp.zeros((LANES - 2, CHUNK), F32)], axis=0
    ).T
    scale = jnp.broadcast_to(columns[:, 0:1], (CHUNK, LANES))
    inner = jnp.broadcast_to(columns[:, 1:2], (CHUNK, LANES))
    for tile in range(width // LANES):
        lanes = slice(tile * LANES, (tile + 1) * LANES)
        at = tile * LANES % half
        back = backs[tile * LANES // half][:, at : at + LANES]
        gain = gain_ref[5:6, lanes]
        z = z_ref[0, :, lanes].astype(F32)
        gate = sigmoid(z)
        gated = z * gate
        y = y_ref[0, :, lanes].astype(F32)
        mixed = y * gated
        scaled_mixed = mixed * scale
        hidden_ref[0, :, lanes] = (scaled_mixed * gain).astype(BF16)
        gain_grad_ref[0:1, lanes] += jnp.sum(back * scaled_mixed, axis=0, keepdims=True)
        grad_mixed = scale * (back * gain) - mixed * inner
        grad_y_ref[0, :, lanes] = (grad_mixed * gated).astype(BF16)
        dz = (grad_mixed * y * (gate + gated * (1.0 - gate))).astype(BF16)
        if tile * LANES < half:
            own_grad_ref[0, :, at : at + LANES] = dz
        else:
            other_grad_ref[0, :, at : at + LANES] = dz


def mixer_backward_kernel(
    scalars,
    grad_y_ref,
    gate_own_grad_ref,
    gate_other_grad_ref,
    own_ref,
    other_ref,
    gate_own_ref,
    gate_other_ref,
    step_ref,
    norm_ref,
    taps_ref,
    head_ref,
    gain_grad_ref,
    slots_ref,
    conv_ref,
    input_ref,
    raw_ref,
    state_ref,
    *rest,
):
    back_refs = rest[:8]
    (
        own_grad_ref,
        other_grad_ref,
        small_grad_ref,
        step_grad,
        grad_state,
        grad_conv,
        step_wide,
        start_wide,
        end_wide,
        from_state,
        to_state,
        end_x,
        start_dy,
        sum_end,
        sum_start,
        sum_step,
        grad_inter,
    ) = rest[8:]
    rows_grad_ref = small_grad_ref.at[0:24]
    wide_grad_ref = small_grad_ref.at[24:32]
    turn = pl.program_id(0)
    chunk = pl.num_programs(0) - 1 - turn
    side, first_end, second_end = scalars[0], scalars[1], scalars[2]
    base = chunk * CHUNK
    width = end_x.shape[1]
    half = width // 2

    @pl.when(turn == 0)
    def _():
        grad_state[...] = jnp.zeros_like(grad_state)
        grad_conv[CHUNK:, :] = jnp.zeros((8, grad_conv.shape[1]), F32)
        small_grad_ref[...] = jnp.zeros_like(small_grad_ref)

    pre, step, log_decay, total, start, ending, kept = decays(
        raw_ref[0], head_ref, base, first_end, second_end, chunk
    )
    expander = head_expander(width)
    step_wide[...] = spread(step, expander)
    start_wide[...] = spread(start, expander)
    end_wide[...] = spread(ending, expander)
    kept_wide = spread(jnp.broadcast_to(kept, (8, LANES)), expander)[0:1]
    skip = spread(jnp.broadcast_to(head_ref[2:3, :], (8, LANES)), expander)[0:1]
    total_rows = total.T

    def activated(lanes):
        conv = conv_ref[0, :, lanes].astype(F32)
        gate = sigmoid(conv)
        value = conv * gate
        return value, gate + value * (1.0 - gate)

    b_lanes, c_lanes = slice(width, width + STATE), slice(width + STATE, width + 2 * STATE)
    b_f32, b_slope = activated(b_lanes)
    c_f32, c_slope = activated(c_lanes)
    b_low, c_low = b_f32.astype(BF16), c_f32.astype(BF16)
    state_low = state_ref[0]
    grad_state_low = grad_state[...].astype(BF16)
    from_state[...] = dot(c_low, state_low)
    to_state[...] = dot(b_low, grad_state_low)
    inter = dot_nt(b_low, c_low)

    def same_pairs(row_at, col_at):
        same, row_ids, col_ids = same_block(base + row_at, base + col_at, first_end, second_end)
        if row_at == col_at:
            same = same & (row_ids <= col_ids)
        return same

    same_00, same_01, same_11 = same_pairs(0, 0), same_pairs(0, HALF), same_pairs(HALF, HALF)
    inter_00 = jnp.where(same_00, inter[:HALF, :HALF], 0.0)
    inter_01 = jnp.where(same_01, inter[:HALF, HALF:], 0.0)
    inter_11 = jnp.where(same_11, inter[HALF:, HALF:], 0.0)
    low_lanes = iota((CHUNK, LANES), 1) < 64
    lane_ids = iota((CHUNK, LANES), 1)
    row_ids = iota((LANES, CHUNK), 0)
    col_sums = jnp.zeros((CHUNK, LANES), F32)
    row_sum_list = []
    grad_inter[...] = jnp.zeros_like(grad_inter)
    for tile in range(width // LANES):
        lanes = slice(tile * LANES, (tile + 1) * LANES)
        values, slope = activated(lanes)
        scaled = values * step_wide[:, lanes]
        scaled_low = scaled.astype(BF16)
        dy_low = grad_y_ref[0, :, lanes]
        dy = dy_low.astype(F32)
        top, bottom = [], []
        for side_at in range(2):
            head = 2 * tile + side_at
            picked = low_lanes if side_at == 0 else ~low_lanes
            lhs = jnp.where(picked, scaled, 0.0).astype(BF16)
            pair_grad = dot_nt(lhs, dy_low)
            column = total[:, head : head + 1]
            row = total_rows[head : head + 1, :]
            top_col, low_col = column[:HALF], column[HALF:]
            top_row, low_row = row[:, :HALF], row[:, HALF:]
            decay_00 = jnp.exp2(jnp.minimum(top_row - top_col, 0.0))
            decay_01 = jnp.exp2(low_row - top_col)
            decay_11 = jnp.exp2(jnp.minimum(low_row - low_col, 0.0))
            part_00 = pair_grad[:HALF, :HALF] * decay_00
            part_01 = pair_grad[:HALF, HALF:] * decay_01
            part_11 = pair_grad[HALF:, HALF:] * decay_11
            grad_inter[:HALF, :HALF] += part_00
            grad_inter[:HALF, HALF:] += part_01
            grad_inter[HALF:, HALF:] += part_11
            full_00, full_01, full_11 = part_00 * inter_00, part_01 * inter_01, part_11 * inter_11
            top.append((inter_00 * decay_00).astype(BF16))
            top.append((inter_01 * decay_01).astype(BF16))
            bottom.append((inter_11 * decay_11).astype(BF16))
            col_sum = jnp.concatenate(
                [
                    jnp.sum(full_00 + full_01, axis=1, keepdims=True),
                    jnp.sum(full_11, axis=1, keepdims=True),
                ],
                axis=0,
            )
            col_sums = jnp.where(lane_ids == head, col_sum, col_sums)
            row_sum_list.append(
                jnp.concatenate(
                    [
                        jnp.sum(full_00, axis=0, keepdims=True),
                        jnp.sum(full_01 + full_11, axis=0, keepdims=True),
                    ],
                    axis=1,
                )
            )
        dy_parts = [
            jnp.where(low_lanes, dy, 0.0).astype(BF16),
            jnp.where(low_lanes, 0.0, dy).astype(BF16),
        ]
        local_top = dot(jnp.concatenate(top, axis=1), jnp.concatenate(dy_parts, axis=0))
        local_bottom = dot(
            jnp.concatenate(bottom, axis=1),
            jnp.concatenate([dy_parts[0][HALF:], dy_parts[1][HALF:]], axis=0),
        )
        local = jnp.concatenate([local_top, local_bottom], axis=0)
        tail = end_wide[:, lanes]
        back_state = to_state[:, lanes]
        grad_scaled = local + tail * back_state
        ended = scaled * tail
        end_x[:, lanes] = ended.astype(BF16)
        sum_end[:, lanes] = (ended * back_state).astype(BF16)
        started = dy * start_wide[:, lanes]
        start_dy[:, lanes] = started.astype(BF16)
        sum_start[:, lanes] = (started * from_state[:, lanes]).astype(BF16)
        sum_step[:, lanes] = (grad_scaled * values).astype(BF16)
        grad_values = step_wide[:, lanes] * grad_scaled + skip[:, lanes] * dy
        wide_grad_ref[6:7, lanes] += jnp.sum(dy * values, axis=0, keepdims=True)
        grad_conv[:CHUNK, lanes] = grad_values * slope

    grad_inter_00 = jnp.where(same_00, grad_inter[:HALF, :HALF], 0.0)
    grad_inter_01 = jnp.where(same_01, grad_inter[:HALF, HALF:], 0.0)
    grad_inter_11 = jnp.where(same_11, grad_inter[HALF:, HALF:], 0.0)
    pair_t = jnp.concatenate(
        [
            jnp.concatenate([grad_inter_00, grad_inter_01], axis=1),
            jnp.concatenate([jnp.zeros((HALF, HALF), F32), grad_inter_11], axis=1),
        ],
        axis=0,
    )
    grad_b = dot(pair_t.astype(BF16), c_low) + dot_nt(end_x[...], grad_state_low)
    grad_c = dot(pair_t.T.astype(BF16), b_low) + dot_nt(start_dy[...], state_low)
    grad_conv[:CHUNK, b_lanes] = grad_b * b_slope
    grad_conv[:CHUNK, c_lanes] = grad_c * c_slope

    folder = head_folder(width)
    end_sums = dot(sum_end[...], folder)
    start_sums = dot(sum_start[...], folder)
    step_sums = dot(sum_step[...], folder)
    state_pairs = jnp.sum(grad_state[...] * state_low.astype(F32), axis=0, keepdims=True)
    first, second = pieces(jnp.broadcast_to(state_pairs, (8, width)), 2)
    state_sums = (dot(first, folder) + dot(second, folder))[0:1] * kept
    row_sums = jnp.concatenate(
        row_sum_list + [jnp.zeros((LANES - len(row_sum_list), CHUNK), F32)], axis=0
    ).T
    grad_total = row_sums - col_sums + start_sums - end_sums
    last = state_sums + jnp.sum(end_sums, axis=0, keepdims=True)
    grad_total = grad_total + jnp.where(iota((CHUNK, LANES), 0) == CHUNK - 1, last, 0.0)
    grad_decay = dot_exact(upper_ones(), grad_total)
    grad_step = step_sums - grad_decay * jnp.exp(head_ref[1:2, :])
    grad_raw = grad_step * sigmoid(pre)
    wide_grad_ref[7:8, :LANES] += jnp.sum(grad_raw, axis=0, keepdims=True)
    wide_grad_ref[7:8, LANES : 2 * LANES] += jnp.sum(grad_decay * log_decay, axis=0, keepdims=True)
    step_grad[...] = grad_raw.astype(BF16)
    rows_grad_ref[0:16, :] += dot(grad_raw.T[0:16, :].astype(BF16), slots_ref[0])
    grad_state[...] = kept_wide * grad_state[...] + dot(c_f32.T.astype(BF16), start_dy[...])

    rows = base + iota((CHUNK, LANES), 0)
    segment = segment_of(rows, first_end, second_end)
    masks = [
        (segment_of(rows + lag, first_end, second_end) == segment).astype(F32)
        for lag in range(1, 4)
    ]
    for tile in range((width + 2 * STATE) // LANES):
        lanes = slice(tile * LANES, (tile + 1) * LANES)
        inputs = input_ref[0, :, lanes].astype(F32)
        current = grad_conv[:CHUNK, lanes]
        found = taps_ref[3:4, lanes] * current
        wide_grad_ref[4:5, lanes] += jnp.sum(current, axis=0, keepdims=True)
        wide_grad_ref[3:4, lanes] += jnp.sum(current * inputs, axis=0, keepdims=True)
        for lag in range(1, 4):
            shifted = grad_conv[lag : lag + CHUNK, lanes] * masks[lag - 1]
            found = found + taps_ref[3 - lag : 4 - lag, lanes] * shifted
            wide_grad_ref[3 - lag : 4 - lag, lanes] += jnp.sum(
                shifted * inputs, axis=0, keepdims=True
            )
        found = found.astype(BF16)
        if tile * LANES < half:
            own_grad_ref[0, :, lanes] = found
        elif tile * LANES < width:
            other_grad_ref[0, :, tile * LANES - half : (tile + 1) * LANES - half] = found
        elif tile * LANES == width:
            shared_b = found
        else:
            own_grad_ref[0, :, half:] = jnp.where(side == 0, shared_b, found)
            other_grad_ref[0, :, half:] = jnp.where(side == 0, found, shared_b)
    grad_conv[CHUNK:, :] = grad_conv[0:8, :]
    shared, offset = half + STATE, gate_own_ref.shape[1] - half
    back = (
        dot_nt(own_grad_ref[0], own_ref[:, :shared])
        + dot_nt(other_grad_ref[0], other_ref[:, :shared])
        + dot(step_grad[...], padded_step(step_ref))
        + dot_nt(gate_own_grad_ref[0], gate_own_ref[:, offset:])
        + dot_nt(gate_other_grad_ref[0], gate_other_ref[:, offset:])
    )
    for tile in range(back.shape[1] // LANES):
        lanes = slice(tile * LANES, (tile + 1) * LANES)
        products = back[:, lanes] * slots_ref[0, :, lanes].astype(F32)
        rows_grad_ref[16:17, lanes] += jnp.sum(products, axis=0, keepdims=True)

    @pl.when(turn == pl.num_programs(0) - 1)
    def _():
        rows_grad_ref[16:17, :] = rows_grad_ref[16:17, :] / norm_ref[0:1, :]
        wide_grad_ref[5:6, :width] = gain_grad_ref[0:1, :]
        heads = width // 64
        wide = wide_grad_ref[...]
        turned = jnp.concatenate([wide[:7, half:width], wide[:7, :half]], axis=1)
        wide_grad_ref[0:7, :width] = jnp.where(side == 0, wide[:7, :width], turned)
        for lanes in (slice(0, LANES), slice(LANES, 2 * LANES)):
            row = wide_grad_ref[7:8, lanes]
            turned = jnp.where(
                iota((1, LANES), 1) < heads // 2,
                pltpu.roll(row, LANES - heads // 2, axis=1),
                pltpu.roll(row, heads // 2, axis=1),
            )
            wide_grad_ref[7:8, lanes] = jnp.where(side == 0, row, turned)
        rows = rows_grad_ref[0:16, :]
        turned = jnp.concatenate(
            [rows[heads // 2 : heads], rows[: heads // 2], rows[heads:]], axis=0
        )
        rows_grad_ref[0:16, :] = jnp.where(side == 0, rows, turned)

    put_rows(back_refs, back, chunk ^ scalars[3])


def whole(shape):
    return pl.BlockSpec(shape, lambda i, s: (0,) * len(shape))


def forward_slot(cols, height=CHUNK):
    return pl.BlockSpec((1, height, cols), lambda i, s: (i ^ s[3], 0, 0))


def same_slot(cols, height=CHUNK):
    return pl.BlockSpec((1, height, cols), lambda i, s: (i, 0, 0))


def low(*shape):
    return jax.ShapeDtypeStruct(shape, BF16)


def full(*shape):
    return jax.ShapeDtypeStruct(shape, F32)


def call(kernel, name, count, scalars, inputs, outputs, scratch=(), events=(), cost=100):
    taken = len(inputs)

    def body(scalars, *refs):
        kernel(scalars, *refs[:taken], *refs[taken + len(events) :])

    anywhere = pl.BlockSpec(memory_space=pl.ANY)
    return pl.pallas_call(
        body,
        grid_spec=pltpu.PrefetchScalarGridSpec(
            num_scalar_prefetch=1,
            grid=(count,),
            in_specs=[spec for _, spec in inputs] + [anywhere] * len(events),
            out_specs=[spec for _, spec in outputs],
            scratch_shapes=list(scratch),
        ),
        out_shape=[shape for shape, _ in outputs],
        compiler_params=pltpu.CompilerParams(vmem_limit_bytes=VMEM_LIMIT),
        cost_estimate=pl.CostEstimate(
            flops=cost * 1_000_000_000, bytes_accessed=1, transcendentals=0
        ),
        name=name,
    )(scalars, *[array for array, _ in inputs], *events)


def constants(*arrays):
    return [(array, whole(array.shape)) for array in arrays]


def run_mixer(scalars, blocks, weights, events=()):
    count = 4
    depth = blocks[0].shape[1]
    joined = weights["wide"].shape[1]
    width = joined - 2 * STATE
    inputs = constants(
        *blocks,
        weights["own"],
        weights["other"],
        weights["step"],
        weights["norm"],
        weights["wide"],
        weights["head"],
    )
    outputs = [
        (low(count, CHUNK, depth), forward_slot(depth)),
        (low(count, CHUNK, joined), forward_slot(joined)),
        (low(count, CHUNK, joined), forward_slot(joined)),
        (low(count, CHUNK, width), forward_slot(width)),
        (full(count, CHUNK, LANES), forward_slot(LANES)),
        (low(count, STATE, width), forward_slot(width, STATE)),
    ]
    scratch = [
        pltpu.VMEM((CHUNK, depth), BF16),
        pltpu.VMEM((CHUNK + 8, joined), F32),
        pltpu.VMEM((STATE, width), F32),
        pltpu.VMEM((CHUNK, width), BF16),
    ] + [pltpu.VMEM((CHUNK, width), F32)] * 4
    return call(
        mixer_kernel, "mixer", count, scalars, inputs, outputs, scratch, events=events
    )


def run_gate(scalars, slots, y, weights, events=()):
    count, _, depth = slots.shape
    width = y.shape[2]
    inputs = (
        [(slots, same_slot(depth))]
        + constants(weights["gate_own"], weights["gate_other"], weights["wide"])
        + [(y, same_slot(width))]
    )
    outputs = [
        (low(count, CHUNK, width), same_slot(width)),
        (low(count, CHUNK, width), same_slot(width)),
        (full(8, count * CHUNK), pl.BlockSpec((8, CHUNK), lambda i, s: (0, i ^ s[3]))),
    ]
    return call(gate_kernel, "gate", count, scalars, inputs, outputs, events=events, cost=20)


def run_project(scalars, hidden, weights, grads=None, events=()):
    count, _, width = hidden.shape
    depth = weights["out_own"].shape[1]
    inputs = [(hidden, same_slot(width))] + constants(weights["out_own"], weights["out_other"])
    if grads is None:
        outputs = [(low(CHUNK, depth // 2), whole((CHUNK, depth // 2)))] * 8
    else:
        inputs.append((grads, forward_slot(depth)))
        outputs = [(low(CHUNK, depth), whole((CHUNK, depth)))] * 4 + [
            (full(8, count * CHUNK), pl.BlockSpec((8, CHUNK), lambda i, s: (0, i ^ s[3])))
        ]
    return call(
        project_kernel,
        "project",
        count,
        scalars,
        inputs,
        outputs,
        events=events,
        cost=1 if grads is None else 20,
    )


def run_gate_backward(scalars, grads, row_values, weights, z, y, inner_total, events=()):
    count, _, width = z.shape
    half = width // 2
    if len(grads) == 2:
        inputs = [(back, forward_slot(half)) for back in grads]
    else:
        inputs = constants(*grads, weights["out_own"], weights["out_other"])
    inputs = (
        inputs
        + [(row_values, pl.BlockSpec((8, CHUNK), lambda i, s: (0, i ^ s[3])))]
        + constants(weights["wide"])
        + [(z, same_slot(width)), (y, same_slot(width))]
    )
    outputs = [
        (low(count, CHUNK, half), same_slot(half)),
        (low(count, CHUNK, half), same_slot(half)),
        (low(count, CHUNK, width), forward_slot(width)),
        (low(count, CHUNK, width), same_slot(width)),
        (full(8, width), whole((8, width))),
    ]
    scratch = []
    if len(grads) != 2:
        depth = grads[0].shape[1]
        outputs.append((low(count, CHUNK, depth), forward_slot(depth)))
        scratch.append(pltpu.VMEM((CHUNK, depth), BF16))
        scratch.append(pltpu.VMEM((EXTRA, depth // 2), BF16))
    return call(
        functools.partial(gate_backward_kernel, 1.0 / inner_total),
        "gate_backward",
        count,
        scalars,
        inputs,
        outputs,
        scratch,
        events=events,
        cost=1,
    )


def run_mixer_backward(scalars, grad_y, gate_grads, gain_grad, weights, slots, kept, events=()):
    count, _, width = grad_y.shape
    half = width // 2
    joined = width + 2 * STATE
    depth = slots.shape[2]
    shared = half + STATE
    final = count - 1

    def slot(cols, height=CHUNK):
        return pl.BlockSpec((1, height, cols), lambda i, s: ((final - i) ^ s[3], 0, 0))

    conv, inputs, raw, states = kept
    operands = (
        [(grad_y, slot(width))]
        + [(grad, slot(half)) for grad in gate_grads]
        + constants(
            weights["own"],
            weights["other"],
            weights["gate_own"],
            weights["gate_other"],
            weights["step"],
            weights["norm"],
            weights["wide"],
            weights["head"],
            gain_grad,
        )
        + [(slots, slot(depth)), (conv, slot(joined)), (inputs, slot(joined))]
        + [(raw, slot(LANES)), (states, slot(width, STATE))]
    )
    outputs = [(low(CHUNK, depth // 2), whole((CHUNK, depth // 2)))] * 8 + [
        (low(count, CHUNK, shared), slot(shared)),
        (low(count, CHUNK, shared), slot(shared)),
        (full(32, depth), whole((32, depth))),
    ]
    scratch = (
        [pltpu.VMEM((CHUNK, LANES), BF16)]
        + [pltpu.VMEM((STATE, width), F32), pltpu.VMEM((CHUNK + 8, joined), F32)]
        + [pltpu.VMEM((CHUNK, width), F32)] * 5
        + [pltpu.VMEM((CHUNK, width), BF16)] * 5
        + [pltpu.VMEM((CHUNK, CHUNK), F32)]
    )
    return call(
        mixer_backward_kernel,
        "mixer_backward",
        count,
        scalars,
        operands,
        outputs,
        scratch,
        events=events,
    )


def weight_grad_kernel(pairs, scalars, *refs):
    own_ref, other_ref = refs[-2:]
    at = 0
    for left_at, own_at, other_at in pairs:
        left_ref = refs[left_at]
        rows = left_ref.shape[0] * left_ref.shape[1]
        left = left_ref[...].reshape(rows, left_ref.shape[2])
        if other_at is None:
            both = refs[own_at][...].reshape(rows, refs[own_at].shape[2])
            cols = both.shape[1] // 2
            own, other = both[:, :cols], both[:, cols:]
        else:
            cols = refs[own_at].shape[2]
            own = refs[own_at][...].reshape(rows, cols)
            other = refs[other_at][...].reshape(rows, cols)
        own_ref[:, at : at + cols] = dot_tn(left, own).astype(BF16)
        other_ref[:, at : at + cols] = dot_tn(left, other).astype(BF16)
        at += cols


def run_weight_grad(scalars, slots, grads, rows_out=None, hidden=None, events=(), cost=100):
    inputs, pairs, cols = [], [], 0

    def left(array):
        count, rows, depth = array.shape
        inputs.append((array, pl.BlockSpec((count, rows, depth // 4), lambda i, s: (0, 0, i))))
        return len(inputs) - 1

    if grads:
        at = left(slots)
        for own, other in zip(grads[::2], grads[1::2]):
            inputs.extend(constants(own, other))
            pairs.append((at, len(inputs) - 2, len(inputs) - 1))
            cols += own.shape[2]
    if hidden is not None:
        at = left(rows_out)
        inputs.extend(constants(hidden))
        pairs.append((at, len(inputs) - 1, None))
        cols += hidden.shape[2] // 2
    depth = inputs[0][0].shape[2]
    outputs = [(low(depth, cols), pl.BlockSpec((depth // 4, cols), lambda i, s: (i, 0)))] * 2
    return call(
        functools.partial(weight_grad_kernel, tuple(pairs)),
        "weight_grad",
        4,
        scalars,
        inputs,
        outputs,
        events=events,
        cost=cost,
    )


def early_back_kernel(scalars, grad_ref, own_ref, other_ref, own_back_ref, other_back_ref):
    grad = grad_ref[0]
    own_back_ref[0] = dot_nt(grad, own_ref[...]).astype(BF16)
    other_back_ref[0] = dot_nt(grad, other_ref[...]).astype(BF16)


def run_early_back(scalars, grads, weights, events=()):
    count, rows, depth = grads.shape
    half = weights["out_own"].shape[0]
    inputs = [(grads, same_slot(depth))] + constants(weights["out_own"], weights["out_other"])
    outputs = [(low(count, rows, half), same_slot(half))] * 2
    return call(
        early_back_kernel, "early_back", count, scalars, inputs, outputs, events=events, cost=20
    )


def norm_backward_kernel(scalars, x_ref, norm_ref, grad_ref, left_ref, right_ref, sum_ref, out_ref):
    depth = x_ref.shape[1]
    half = depth // 2
    squares = jnp.zeros((CHUNK, LANES), F32)
    inner = jnp.zeros((CHUNK, LANES), F32)

    def weighted(tile):
        at = tile * LANES
        source = left_ref if at < half else right_ref
        at = at % half
        return source[:, at : at + LANES] * norm_ref[0:1, tile * LANES : (tile + 1) * LANES]

    for tile in range(depth // LANES):
        x = x_ref[:, tile * LANES : (tile + 1) * LANES].astype(F32)
        squares = squares + x * x
        inner = inner + weighted(tile) * x
    scale = lax.rsqrt(jnp.sum(squares, axis=1, keepdims=True) / depth + NORM_EPSILON)
    factor = scale * scale * scale * (jnp.sum(inner, axis=1, keepdims=True) / depth)
    scale = jnp.broadcast_to(scale, (CHUNK, LANES))
    factor = jnp.broadcast_to(factor, (CHUNK, LANES))
    crossed = jnp.zeros((CHUNK, LANES), F32)
    for tile in range(depth // LANES):
        lanes = slice(tile * LANES, (tile + 1) * LANES)
        x = x_ref[:, lanes].astype(F32)
        found = (grad_ref[:CHUNK, lanes].astype(F32) + weighted(tile) * scale - x * factor).astype(BF16)
        out_ref[:CHUNK, lanes] = found
        crossed = crossed + found.astype(F32) * sum_ref[:, lanes]
    ones = jnp.ones((EXTRA, LANES), BF16)
    first, second = pieces(crossed, 2)
    out_ref[CHUNK:, :] = jnp.zeros((EXTRA, depth), BF16)
    out_ref[CHUNK:, : 3 * CHUNK] = jnp.concatenate(
        pieces(dot_nt(ones, first) + dot_nt(ones, second), 3), axis=1
    )


def run_norm_backward(scalars, x, norm, grad, dnormed, summed, events=(), cost=1):
    rows, depth = x.shape
    (found,) = call(
        norm_backward_kernel,
        "norm_backward",
        1,
        scalars,
        constants(x, norm, grad, *dnormed, summed),
        [(low(rows + EXTRA, depth), whole((rows + EXTRA, depth)))],
        events=events,
        cost=cost,
    )
    return found


def crossing(bit):
    return [(i, i ^ bit) for i in range(4)]


def exchange(block, bit):
    return lax.ppermute(block, "tensor", crossing(bit))


def swap_cores(block):
    return lax.ppermute(block, "pipe", [(0, 1), (1, 0)])


def shift_groups(block, distance):
    count = lax.axis_size("fsdp")
    return lax.ppermute(block, "fsdp", [(i, (i + distance) % count) for i in range(count)])


def after(values, *events, cost=0):
    single = not isinstance(values, (tuple, list))
    values = [values] if single else list(values)
    anywhere = pl.BlockSpec(memory_space=pl.ANY)
    found = pl.pallas_call(
        lambda *refs: None,
        out_shape=[jax.ShapeDtypeStruct(v.shape, v.dtype) for v in values],
        in_specs=[anywhere] * (len(values) + len(events)),
        out_specs=[anywhere] * len(values),
        input_output_aliases={at: at for at in range(len(values))},
        cost_estimate=pl.CostEstimate(
            flops=cost * 1_000_000_000, bytes_accessed=1, transcendentals=0
        ),
        name="fence",
    )(*values, *events)
    return found[0] if single else found


def gather_begin(block):
    return block, exchange(block, 1), exchange(block, 2)


def gather_end(begun, *others):
    block, from_1, from_2 = begun
    cols = block.shape[1] // 2
    left, right = from_1[:, :cols], from_2[:, cols:]
    if others:
        left, right = after((left, right), *others)
    left_3, right_3 = exchange(left, 2), exchange(right, 1)
    return [block, from_1, from_2, left_3, right_3]


def scatter_begin(halves):
    left, right = halves[:4], halves[4:]
    left_3, right_3 = exchange(left[3], 2), exchange(right[3], 1)
    right_1, left_2 = exchange(right[1], 1), exchange(left[2], 2)
    return left, right, left_3, right_3, right_1, left_2


def scatter_middle(begun, *others):
    left, right, left_3, right_3, right_1, left_2 = begun
    if others:
        left_3, right_3 = after((left_3, right_3), *others)
    left_1 = (left[1].astype(F32) + left_3.astype(F32)).astype(BF16)
    right_2 = (right[2].astype(F32) + right_3.astype(F32)).astype(BF16)
    sent = (left_1, right_2)
    left_1, right_2 = exchange(left_1, 1), exchange(right_2, 2)
    return (left[0], left_1, left_2, right[0], right_1, right_2), sent


def scatter_end(middle, *others):
    left_0, left_1, left_2, right_0, right_1, right_2 = middle
    if others:
        left_0 = after(left_0, *others)
    return (
        left_0.astype(F32) + left_1.astype(F32) + left_2.astype(F32),
        right_0.astype(F32) + right_1.astype(F32) + right_2.astype(F32),
    )


def sum_tensor(value):
    return value + exchange(value, 1) + exchange(value, 2) + exchange(value, 3)


def sum_groups(value, part):
    count = lax.axis_size("fsdp")
    bit = 2 if part else 1
    while bit < (count if part else 2):
        value = value + lax.ppermute(value, "fsdp", [(i, i ^ bit) for i in range(count)])
        bit *= 2
    return value


def spread_parts(value, axis_name):
    count, at = lax.axis_size(axis_name), lax.axis_index(axis_name)
    parts = [lax.dynamic_index_in_dim(value, at, 0, keepdims=False)]
    for distance in range(1, count):
        block = lax.dynamic_index_in_dim(value, (at + distance) % count, 0, keepdims=False)
        pairs = [(i, (i + distance) % count) for i in range(count)]
        parts.append(lax.ppermute(block, axis_name, pairs))
    return parts


def add_up(parts):
    total = parts[0].astype(F32)
    for part in parts[1:]:
        total = total + part.astype(F32)
    return total.astype(parts[0].dtype)


def gather_groups_begin(block):
    return [block] + [shift_groups(block, k) for k in range(1, lax.axis_size("fsdp"))]


def gather_groups_end(found, axis):
    count, place = lax.axis_size("fsdp"), lax.axis_index("fsdp")
    size = found[0].shape[axis]
    shape = list(found[0].shape)
    shape[axis] = size * count
    total = jnp.zeros(shape, found[0].dtype)
    for distance, piece in enumerate(found):
        total = lax.dynamic_update_slice_in_dim(
            total, piece, (place - distance) % count * size, axis
        )
    return total


def gather_groups(block, axis):
    return gather_groups_end(gather_groups_begin(block), axis)


def ring_groups(block, rows, waits):
    count, place = lax.axis_size("fsdp"), lax.axis_index("fsdp")
    cols = block.shape[1]
    found = jnp.zeros((rows * count, cols), block.dtype)
    packed = jnp.zeros((count, block.shape[0] - rows, cols), block.dtype)

    def put(totals, piece, at, col):
        found, packed = totals
        found = lax.dynamic_update_slice(found, piece[:rows], (at % count * rows, col))
        packed = lax.dynamic_update_slice(packed, piece[rows:][None], (at % count, 0, col))
        return found, packed

    totals = put((found, packed), block, place, 0)
    up, down = block[:, : cols // 2], block[:, cols // 2 :]
    steps = []
    for distance in range(1, count):
        if distance in waits:
            up, down = after((up, down), *waits[distance])
        up, down = shift_groups(up, 1), shift_groups(down, -1)
        steps.append(up)
        totals = put(totals, up, place - distance, 0)
        totals = put(totals, down, place + distance, cols // 2)
    return totals, steps


def rms_scale(x):
    return lax.rsqrt(jnp.mean(x * x, axis=1, keepdims=True) + NORM_EPSILON)


def channel_places(count, depth, head_count, head_size):
    size, slice_size = depth // count, head_size // count
    shared = 2 * STATE // count
    width = head_count * head_size
    places = np.zeros((depth, width + 2 * STATE), np.float32)
    for group in range(count):
        for head in range(head_count):
            for at in range(slice_size):
                lane = group * size + head * slice_size + at
                places[lane, head * head_size + group * slice_size + at] = 1
        for at in range(shared):
            lane = group * size + head_count * slice_size + at
            places[lane, width + group * shared + at] = 1
    return places


def shards(
    tokens,
    out_grad,
    seq_lengths,
    norm_gain,
    w_zx,
    w_bc,
    w_dt,
    conv_x,
    conv_bc,
    out_gain,
    head_params,
    out_weight,
):
    core = lax.axis_index("pipe")
    place = lax.axis_index("tensor")
    is_first = core == 0
    fsdp_count = lax.axis_size("fsdp")
    fsdp_at = lax.axis_index("fsdp")
    tensor_count = lax.axis_size("tensor")
    local_depth = norm_gain.shape[1]
    depth = local_depth * fsdp_count
    width = w_zx.shape[3]
    half = width // 2
    head_count = w_dt.shape[2]
    head_size = width // head_count
    local_head = conv_x.shape[3]
    local_wide = head_count * local_head
    inner_total = width * tensor_count
    joined = width + 2 * STATE
    local_rows = tokens.shape[1]
    tap_rows = conv_x.shape[1]
    places = jnp.asarray(
        channel_places(fsdp_count, depth, head_count, head_size), BF16
    )

    def by_core(first, second):
        return jnp.where(is_first, first, second)

    def local_order(value):
        size = value.shape[-1] // 2
        return by_core(
            value, jnp.concatenate([value[..., size:], value[..., :size]], axis=-1)
        )

    def micro(array):
        return lax.dynamic_index_in_dim(array, core, 0, keepdims=False)

    def pad_to(value, rows, cols):
        return jnp.pad(value, ((0, rows - value.shape[0]), (0, cols - value.shape[1])))

    lengths = lax.dynamic_index_in_dim(seq_lengths, core, 0, keepdims=False)[0]
    scalars = jnp.stack([core, lengths[0], lengths[0] + lengths[1], place]).astype(jnp.int32)

    heads, left_over = [], head_params[0]
    for _ in range(3):
        part = lax.reduce_precision(left_over, 8, 7)
        heads.append(part.astype(BF16))
        left_over = left_over - part
    heads = jnp.concatenate(heads)
    packed = jnp.concatenate(
        [
            pad_to(w_dt[0].T, 16, local_depth),
            pad_to(
                jnp.concatenate([conv_x[0].reshape(tap_rows, local_wide), conv_bc[0]], axis=1),
                tap_rows,
                local_depth,
            ),
            pad_to(out_gain[0].reshape(1, local_wide), 1, local_depth),
            norm_gain,
            pad_to(heads, 16 - tap_rows - 2, local_depth),
        ]
    )

    def shared_half(which):
        weights = jnp.concatenate(
            [
                lax.dynamic_slice(w_zx, (0, 0, 1, which * half), (1, local_depth, 1, half))[
                    0, :, 0
                ],
                lax.dynamic_slice_in_dim(w_bc[0], which * STATE, STATE, 1),
            ],
            axis=1,
        )
        rows = lax.dynamic_slice_in_dim(packed, which * 16, 16, 0)
        return jnp.concatenate([weights, pad_to(rows, 16, half + STATE)])

    def gate_half(which):
        return lax.dynamic_slice(w_zx, (0, 0, 0, which * half), (1, local_depth, 1, half))[
            0, :, 0
        ]

    def out_half(which):
        return lax.dynamic_slice_in_dim(out_weight[0], which * half, half, 0)

    shared_theirs = swap_cores(shared_half(1 - core))
    begun = gather_begin(micro(tokens))
    shared_mine = shared_half(core)
    first, second = {}, {}
    cotangent = micro(out_grad)
    blocks = gather_end(begun)
    natural_cotangent = lax.all_gather(
        after(cotangent, *blocks[3:]), "tensor", axis=0, tiled=True
    ).reshape(-1, CHUNK, depth)
    (first["own"], packed_own), steps = ring_groups(
        jnp.concatenate(
            [
                by_core(shared_mine, shared_theirs),
                by_core(shared_theirs, shared_mine)[local_depth:],
            ]
        ),
        local_depth,
        {2: begun[1:]},
    )
    first["other"] = swap_cores(first["own"])

    packed_other = swap_cores(packed_own)

    def small_weights(weights, own, other):
        steps_part, wide_part = [
            jnp.moveaxis(part[:, :, :local_depth], 0, 1).reshape(16, depth)
            for part in (by_core(own, other), by_core(other, own))
        ]
        wide = dot(wide_part[:8], places)
        weights["wide"] = jnp.concatenate([local_order(wide[:, :width]), wide[:, width:]], axis=1)
        weights["step"] = by_core(
            steps_part,
            jnp.concatenate(
                [
                    steps_part[head_count // 2 : head_count],
                    steps_part[: head_count // 2],
                    steps_part[head_count:],
                ]
            ),
        )
        weights["norm"] = wide_part[tap_rows + 1 : tap_rows + 9].astype(F32)
        heads = wide_part[tap_rows + 2 :, :head_count].astype(F32).reshape(3, 3, head_count)
        weights["head"] = pad_to(local_order(heads[0] + (heads[1] + heads[2])), 8, LANES)

    small_weights(first, packed_own[:, :16], packed_other[:, :16])
    small_weights(second, packed_own[:, 16:], packed_other[:, 16:])

    gate_mine, gate_theirs = gate_half(core), gate_half(1 - core)
    out_mine, out_theirs = out_half(core), out_half(1 - core)
    if local_depth == half:
        both = swap_cores(
            after(jnp.concatenate([gate_theirs, out_theirs], axis=1), *begun[1:])
        )
        gate_theirs, out_theirs = both[:, :half], both[:, half:]
    else:
        gate_theirs, out_theirs = swap_cores(gate_theirs), swap_cores(out_theirs)
    gate_begun = gather_groups_begin(after(by_core(gate_mine, gate_theirs), steps[-1]))

    slots, conv, inputs, y, raw, states = run_mixer(scalars, blocks, first)
    kept_first = (conv, inputs, raw, states)
    first["gate_own"] = gather_groups_end(after(gate_begun, y), 0)
    first["gate_other"] = swap_cores(first["gate_own"])
    out_block = after(by_core(out_mine, out_theirs), y, *gate_begun[1:])
    out_begun = gather_groups_begin(out_block)
    z, hidden, sums = run_gate(scalars, slots, y, first)
    joined_block = after(
        jnp.concatenate(
            [
                by_core(shared_theirs, shared_mine)[:local_depth],
                by_core(gate_theirs, gate_mine),
            ],
            axis=1,
        ),
        hidden,
        *out_begun[1:],
    )
    joined_second = lax.all_gather(joined_block, "fsdp", axis=0, tiled=True)
    second["out_own"] = lax.all_gather(
        after(by_core(out_theirs, out_mine), joined_block), "fsdp", axis=1, tiled=True
    )
    first_saved = (slots, z, y)
    sums = sum_tensor(sums[:1])[0]
    scale_first = lax.rsqrt(sums / inner_total + NORM_EPSILON)
    own_scale = lax.dynamic_slice_in_dim(scale_first, place * local_rows, local_rows, 0)
    first["out_own"] = gather_groups_end(after(out_begun, hidden), 1)
    first["out_other"] = swap_cores(first["out_own"])
    outputs = run_project(scalars, hidden, first, events=(scale_first, natural_cotangent))
    scatter_state, _ = scatter_middle(scatter_begin(outputs))
    summed = jnp.concatenate(scatter_end(scatter_state), axis=1)
    x_0 = micro(tokens).astype(F32)
    y_first = (x_0 + summed * own_scale[:, None]).astype(BF16)
    begun = gather_begin(y_first)
    joined_second = after(joined_second, *begun[1:])
    second["own"] = second["gate_own"] = joined_second
    second["other"] = second["gate_other"] = swap_cores(joined_second)
    blocks = gather_end(begun)

    slots, conv, inputs, y, raw, states = run_mixer(scalars, blocks, second)
    kept_second = (conv, inputs, raw, states)
    second["out_own"] = after(second["out_own"], y)
    second["out_other"] = swap_cores(second["out_own"])
    z, hidden_second, squares = run_gate(scalars, slots, y, second)
    *outputs, crossed = run_project(
        scalars, hidden_second, second, natural_cotangent
    )
    sums = sum_tensor(jnp.concatenate([squares[:1], crossed[:1]]))
    early_backs = run_early_back(
        scalars, natural_cotangent, second, events=(crossed,)
    )
    scale_second = lax.rsqrt(sums[0] / inner_total + NORM_EPSILON)
    own_scale = lax.dynamic_slice_in_dim(scale_second, place * local_rows, local_rows, 0)

    def both_micros(one, two):
        keep, send = by_core(one, two), by_core(two, one)
        got = swap_cores(send)
        return jnp.stack([by_core(keep, got), by_core(got, keep)])[None]

    def both_halves(one, two):
        keep, send = by_core(one, two), by_core(two, one)
        got = swap_cores(send)
        return by_core(keep, got), by_core(got, keep)

    def add_cores(own, got):
        return (own.astype(F32) + got.astype(F32)).astype(BF16)

    def rows_of(value):
        return value.reshape(-1, value.shape[-1])

    own_gate, other_gate, hidden, grad_y, gain_grad = run_gate_backward(
        scalars,
        early_backs,
        jnp.pad(jnp.stack([scale_second, sums[1]]), ((0, 6), (0, 0))),
        second,
        z,
        y,
        inner_total,
    )
    y_parts = [
        exchange(part, at) for at, part in zip(range(1, 4), after(outputs[1:], sums))
    ]
    *backs, own_grad, other_grad, small_second = run_mixer_backward(
        scalars, grad_y, [own_gate, other_gate], gain_grad, second, slots, kept_second
    )
    scatter_state = scatter_begin(backs)
    in_own, in_other = run_weight_grad(
        scalars, slots, [own_gate, other_gate, own_grad, other_grad], events=y_parts
    )
    scatter_state, sent = scatter_middle(scatter_state, in_other)
    in_other = after(in_other, *sent)
    in_sum = add_cores(in_own, swap_cores(in_other))
    in_second = in_sum[:, :width]
    shared_second = in_sum[:, width:]
    dnormed = scatter_end(scatter_state, in_second)
    in_second = lax.psum_scatter(in_second, "fsdp", scatter_dimension=0, tiled=True)
    grad_second = run_norm_backward(
        scalars, y_first, second["norm"], cotangent, dnormed, summed
    )
    begun = gather_begin(grad_second)
    out_own, out_other = run_weight_grad(
        scalars, None, [], natural_cotangent, hidden, events=(grad_second,)
    )
    out_other, from_1, from_2 = after((out_other, *begun[1:]))
    blocks = gather_end((begun[0], from_1, from_2))
    out_own_second = out_own

    slots, z, y = first_saved
    own_gate, other_gate, hidden, grad_y, gain_grad, grads = run_gate_backward(
        scalars,
        blocks,
        jnp.pad(scale_first[None], ((0, 7), (0, 0))),
        first,
        z,
        y,
        inner_total,
    )
    out_sum = add_cores(out_own_second, swap_cores(after(out_other, grad_y)))
    out_second = lax.psum_scatter(out_sum, "fsdp", scatter_dimension=0, tiled=True)
    gate_own, gate_other = run_weight_grad(
        scalars, slots, [own_gate, other_gate], grads, hidden, events=(in_second,), cost=1
    )
    gate_sum = add_cores(gate_own, swap_cores(gate_other))
    gate_first = lax.psum_scatter(gate_sum, "fsdp", scatter_dimension=0, tiled=True)
    *backs, own_grad, other_grad, small_first = run_mixer_backward(
        scalars,
        grad_y,
        [own_gate, other_gate],
        gain_grad,
        first,
        slots,
        kept_first,
        events=(gate_sum,),
    )
    left, right, left_3, right_3, right_1, left_2 = scatter_begin(backs)
    ours = by_core(small_first, small_second) + swap_cores(by_core(small_second, small_first))
    shared_own, shared_other = run_weight_grad(
        scalars, slots, [own_grad, other_grad], cost=1
    )
    left_3, right_3, ours, shared_other = after((left_3, right_3, ours, shared_other))
    left_1 = exchange((left[1].astype(F32) + left_3.astype(F32)).astype(BF16), 1)
    right_2 = exchange((right[2].astype(F32) + right_3.astype(F32)).astype(BF16), 2)
    shared_got = swap_cores(shared_other)
    ours = sum_groups(ours, 0)
    shared_sum = add_cores(shared_own, shared_got)
    conv_sum = after(shared_sum[:, :half], gate_first, out_second)
    conv_first = lax.psum_scatter(conv_sum, "fsdp", scatter_dimension=0, tiled=True)
    ours, shared_sum = after((ours, shared_sum[:, half:]), conv_sum)
    shared_low, shared_high = both_halves(shared_sum, shared_second)
    total = sum_groups(ours, 1)
    dnormed = scatter_end((left[0], left_1, left_2, right[0], right_1, right_2))
    grad_first = run_norm_backward(
        scalars,
        lax.dynamic_index_in_dim(tokens, core, 0, keepdims=False),
        first["norm"],
        grad_second,
        dnormed,
        summed,
    )
    grad_bc = jnp.concatenate([shared_low, shared_high], axis=1).reshape(
        fsdp_count, tensor_count, -1, 2 * STATE
    )
    grad_bc, total, grad_first = after((jnp.moveaxis(grad_bc, 1, 0), total, grad_first))
    input_out = both_micros(grad_first, grad_second)[:, :, :local_rows]
    rows = lax.dynamic_slice_in_dim(total[:24], fsdp_at * local_depth, local_depth, 1)
    wide = total[24:, :joined]
    everywhere = sum_tensor(
        jnp.concatenate([rows[16:17], wide[:5, width:].reshape(1, -1)], axis=1)
    )[0]
    grad_bc = add_up(spread_parts(grad_bc, "tensor"))
    grad_bc = add_up(spread_parts(grad_bc, "fsdp"))
    second_parts = jnp.concatenate([in_second[:, :half], out_second], axis=1)
    low_half, high_half = both_halves(after(gate_first, total), second_parts)
    y_summed = after(outputs[0], total).astype(F32)
    for part in y_parts:
        y_summed = y_summed + part.astype(F32)
    y_second = (y_first.astype(F32) + y_summed * own_scale[:, None]).astype(BF16)
    section_out = both_micros(y_first, y_second)
    grad_out_weight = jnp.concatenate(
        [low_half[:, half:].T, high_half[:, half:].T], axis=0
    ).astype(F32)
    conv_low, conv_high = both_halves(conv_first, in_second[:, half:])
    grad_zx = jnp.stack(
        [
            jnp.concatenate([low_half[:, :half], high_half[:, :half]], axis=1),
            jnp.concatenate([conv_low, conv_high], axis=1),
        ],
        axis=1,
    ).astype(F32)

    by_head = lax.dynamic_slice_in_dim(
        wide[:7, :width].reshape(7, head_count, head_size), fsdp_at * local_head, local_head, 2
    )
    grad_heads = jnp.concatenate(
        [
            wide[7:8, :head_count],
            wide[7:8, LANES : LANES + head_count],
            jnp.sum(wide[6, :width].reshape(1, head_count, head_size), axis=2),
        ]
    )
    grad_dt = rows[:head_count].T
    gain_size = local_depth // tensor_count
    grad_gain = lax.dynamic_slice_in_dim(everywhere, place * gain_size, gain_size, 0)
    shared_size = 2 * STATE // (fsdp_count * tensor_count)
    grad_shared = lax.dynamic_slice_in_dim(
        everywhere[local_depth:].reshape(tap_rows, -1), (fsdp_at * tensor_count + place) * shared_size, shared_size, 1
    )
    return (
        section_out,
        input_out,
        grad_gain[None],
        grad_zx[None],
        grad_bc.astype(F32)[None],
        grad_dt[None],
        by_head[:tap_rows][None],
        grad_shared[None],
        by_head[5][None],
        grad_heads[None],
        grad_out_weight[None],
    )


def solution(mesh):
    return jax.shard_map(
        shards,
        mesh=mesh,
        in_specs=(
            P(None, ("fsdp", "tensor"), None),
            P(None, ("fsdp", "tensor"), None),
            P(None, "fsdp", None),
            P("pipe", "fsdp"),
            P("pipe", "fsdp", None, "tensor"),
            P("pipe", "fsdp", None),
            P("pipe", "fsdp", "tensor"),
            P("pipe", None, "tensor", "fsdp"),
            P("pipe", None, "fsdp"),
            P("pipe", "tensor", "fsdp"),
            P("pipe", None, "tensor"),
            P("pipe", "tensor", "fsdp"),
        ),
        out_specs=(
            P("pipe", None, ("fsdp", "tensor"), None),
            P("pipe", None, ("fsdp", "tensor"), None),
            P("pipe", ("fsdp", "tensor")),
            P("pipe", "fsdp", None, "tensor"),
            P("pipe", ("fsdp", "tensor"), None),
            P("pipe", "fsdp", "tensor"),
            P("pipe", None, "tensor", "fsdp"),
            P("pipe", None, ("fsdp", "tensor")),
            P("pipe", "tensor", "fsdp"),
            P("pipe", None, "tensor"),
            P("pipe", "tensor", "fsdp"),
        ),
        check_vma=False,
    )
```
